32 devices in a mesh: groups: 2 (over x), ctx: 16 (over z, y, core).
Axes of the slice: x: 2, y: 2, z: 4, core: 2. Of those that a mesh axis runs over, the one named last changes fastest.
Arguments:
- queries: bfloat16 [2048, 4096], P(('groups', 'ctx')), parts along dimension 0, may hold values from -256 to 256
- text_keys: bfloat16 [2048, 512], P(('groups', 'ctx')), parts along dimension 0, may hold values from -4 to 4
- text_values: bfloat16 [2048, 512], P(('groups', 'ctx')), parts along dimension 0, may hold values from -5 to 5
- image_features: bfloat16 [16384, 256], P(('groups', 'ctx')), parts along dimension 0, may hold values from -300 to 300
- kv_weight: bfloat16 [8192, 1024], P('ctx'), may hold values from -0.0625 to 0.0625
- image_grids: int32 [32, 3], P(('groups', 'ctx')), parts along dimension 0, may hold values from 0 to 58, as said below
Outputs:
- attention: bfloat16 [2048, 4096], P(('groups', 'ctx')), parts along dimension 0
- cache_keys: bfloat16 [2048, 512], P(('groups', 'ctx')), parts along dimension 0
- cache_values: bfloat16 [2048, 512], P(('groups', 'ctx')), parts along dimension 0
The draws below stay inside these ranges and needn't reach their ends.
There are 2 independent parts, one for each index of `groups`. The reference program is written for one: setup_inputs(seed, part) draws one part's arguments, and reference() takes and returns one part's arrays. A program takes and returns all parts, laid end to end along the dimension named above; an argument that names none is the same for every part. Nothing has to cross between parts.
Inputs may be any that keep to these rules, and one draw needn't show every extreme that they name: `image_grids`: row b describes the one image of context shard b: offset o, grid rows gh and grid columns gw with 2 <= gh, gw <= 4; its tokens take positions b * 64 + o to b * 64 + o + gh * gw - 1, token k at grid row k // gw and column k % gw; o + gh * gw <= 62; some shard has a 4 x 4 image.
All inputs are finite; a program needn't handle non-finite values.
Results may differ from the reference program's by a relative error of at most 0.0053.
Values may be sent and summed in bfloat16 or wider, within the bound.
A program may use at most 128 MiB of HBM per device.

```python
import math
import jax
import jax.numpy as jnp
from jax import lax

D = 8192
HEADS = 32
KV_HEADS = 4
HEAD_DIM = 128
GRID = 4
ROWS = 64
CONTEXT = 1024
N_CTX = 16


def image_layout(key):
    base_key = jax.random.fold_in(key, 11)
    tall_key, wide_key, large_key, small_key, offset_key = jax.random.split(base_key, 5)
    grid_tall = jax.random.randint(tall_key, (N_CTX,), 2, GRID + 1, dtype=jnp.int32)
    grid_wide = jax.random.randint(wide_key, (N_CTX,), 2, GRID + 1, dtype=jnp.int32)
    large_shard = jax.random.randint(large_key, (), 0, N_CTX, dtype=jnp.int32)
    small_shard = (large_shard + 1 + jax.random.randint(small_key, (), 0, N_CTX - 1, dtype=jnp.int32)) % N_CTX
    grid_tall = grid_tall.at[large_shard].set(GRID).at[small_shard].set(2)
    grid_wide = grid_wide.at[large_shard].set(GRID).at[small_shard].set(2)
    room_left = ROWS - 2 - grid_tall * grid_wide
    offsets = jax.random.randint(offset_key, (N_CTX,), 0, room_left + 1, dtype=jnp.int32)
    offsets = offsets.at[small_shard].set(room_left[small_shard])
    return (offsets, grid_tall, grid_wide)


def draw_image_grids(key, part):
    offsets, grid_tall, grid_wide = image_layout(key)
    return jnp.stack([offsets, grid_tall, grid_wide], axis=1).astype(jnp.int32)


def base_keys(key):
    noise = jax.random.normal(jax.random.fold_in(key, 21), (ROWS * N_CTX, KV_HEADS * HEAD_DIM), jnp.float32)
    return jnp.clip(noise, -4.0, 4.0)


def draw_text_keys(key, part):
    keys_f32 = base_keys(key)
    return keys_f32.astype(jnp.bfloat16)


def draw_queries(key, part):
    noise = jax.random.normal(jax.random.fold_in(key, 31), (ROWS * N_CTX, HEADS * HEAD_DIM), jnp.float32)
    noise = jnp.clip(noise * 2.5, -10.0, 10.0)
    return noise.astype(jnp.bfloat16)


def draw_image_features(key, part):
    total_slots = GRID * GRID * N_CTX
    feature_key, slot_key, noise_key = jax.random.split(jax.random.fold_in(key, 51), 3)
    ramp = jnp.arange(D, dtype=jnp.float32) / D
    noise = jnp.clip(jax.random.normal(noise_key, (D, total_slots), jnp.float32), -4.0, 4.0)
    feature_scale = jnp.sqrt(1.0 + 2.0 * ramp) * jnp.exp(jax.random.uniform(feature_key, (D,), jnp.float32, -0.6, 0.6))
    slot_scale = 10.0 ** jax.random.uniform(slot_key, (total_slots,), jnp.float32, 0.0, 1.0)
    return (noise * feature_scale[:, None] * slot_scale[None, :]).astype(jnp.bfloat16)


def level_of(key, shape, cuts, least, high):
    level = 1.0
    for axis_at, shards_of in cuts:
        steps = jax.random.uniform(jax.random.fold_in(jax.random.fold_in(key, 6), axis_at), (shards_of,), jnp.float32, least / len(cuts), high / len(cuts))
        level = level * jnp.repeat(jnp.exp(steps), shape[axis_at] // shards_of).reshape((-1,) + (1,) * (len(shape) - 1 - axis_at))
    return level


def scatter_about(rng, dims, deviation, reach, cuts=(), kind=jnp.bfloat16):
    values = deviation * jax.random.normal(rng, dims, jnp.float32)
    if cuts:
        values = values * level_of(rng, dims, cuts, -0.22, 0.18)
    return jnp.clip(values, -reach, reach).astype(kind)


def setup_inputs(seed: int = 0, part: int = 0) -> dict:
    key_of = jax.random.split(jax.random.key(seed), 7)
    own_keys = jax.random.split(jax.random.fold_in(key_of[6], part), 7)
    queries = draw_queries(jax.random.fold_in(jax.random.fold_in(key_of[6], part), 71), part)
    text_keys = draw_text_keys(jax.random.fold_in(jax.random.fold_in(key_of[6], part), 71), part)
    text_values = scatter_about(own_keys[2], (CONTEXT, KV_HEADS * HEAD_DIM), 1.0, 5.0, ((0, 16),))
    image_features = draw_image_features(jax.random.fold_in(jax.random.fold_in(key_of[6], part), 71), part)
    kv_weight = scatter_about(key_of[4], (D, 2 * KV_HEADS * HEAD_DIM), D ** -0.5, 0.0625, ((0, 16),))
    image_grids = draw_image_grids(jax.random.fold_in(jax.random.fold_in(key_of[6], part), 71), part)
    return {"queries": queries, "text_keys": text_keys, "text_values": text_values, "image_features": image_features, "kv_weight": kv_weight, "image_grids": image_grids}


def rope_tables(time_ids, height_ids, width_ids):
    half_dim = HEAD_DIM // 2
    first_bound = HEAD_DIM // 8
    second_bound = first_bound + 3 * HEAD_DIM // 16
    pair_index = jnp.arange(half_dim, dtype=jnp.int32)
    inv_freq = 1000000.0 ** (-(2.0 * pair_index.astype(jnp.float32)) / HEAD_DIM)
    chosen = jnp.where(pair_index[None, :] < first_bound, time_ids[:, None], jnp.where(pair_index[None, :] < second_bound, height_ids[:, None], width_ids[:, None]))
    angles = chosen.astype(jnp.float32) * inv_freq[None, :]
    cosine = jnp.concatenate([jnp.cos(angles), jnp.cos(angles)], axis=1)
    sine_table = jnp.concatenate([jnp.sin(angles), jnp.sin(angles)], axis=1)
    return (cosine, sine_table)

def rotate(key_heads, cosine, sine_table):
    half_dim = HEAD_DIM // 2
    turned = jnp.concatenate([-key_heads[..., half_dim:], key_heads[..., :half_dim]], axis=-1)
    return key_heads * cosine[:, None, :] + turned * sine_table[:, None, :]

def attend(queries, cache_keys, cache_values):
    length = queries.shape[0]
    head_group = HEADS // KV_HEADS
    block_size = math.gcd(length, 256)
    keys_all = cache_keys.astype(jnp.float32).reshape(length, KV_HEADS, HEAD_DIM)
    values_all = cache_values.astype(jnp.float32).reshape(length, KV_HEADS, HEAD_DIM)
    results = []
    for begin_row in range(0, length, block_size):
        end_row = begin_row + block_size
        query_block = queries[begin_row:end_row].astype(jnp.float32).reshape(block_size, KV_HEADS, head_group, HEAD_DIM)
        scores = jnp.einsum('qgmd,kgd->gmqk', query_block, keys_all[:end_row]) / math.sqrt(HEAD_DIM)
        query_pos = begin_row + jnp.arange(block_size, dtype=jnp.int32)
        key_pos = jnp.arange(end_row, dtype=jnp.int32)
        allowed = key_pos[None, :] <= query_pos[:, None]
        scores = jnp.where(allowed, scores, -1e+30)
        largest = lax.optimization_barrier(jnp.max(scores, axis=-1, keepdims=True))
        weights = jnp.where(allowed, jnp.exp(scores - largest), 0.0)
        totals = lax.optimization_barrier(jnp.sum(weights, axis=-1))
        rounded = lax.optimization_barrier(weights.astype(jnp.bfloat16)).astype(jnp.float32)
        blended = jnp.einsum('gmqk,kgd->qgmd', rounded, values_all[:end_row])
        blended = blended / jnp.transpose(totals, (2, 0, 1))[..., None]
        results.append(blended.reshape(block_size, HEADS * HEAD_DIM).astype(jnp.bfloat16))
    return jnp.concatenate(results, axis=0)

def reference(queries, text_keys, text_values, image_features, kv_weight, image_grids):
    kv_width = KV_HEADS * HEAD_DIM
    slot_count = GRID * GRID
    total_slots = slot_count * N_CTX
    raw_kv = jnp.dot(image_features.T, kv_weight, preferred_element_type=jnp.float32)
    feature_f32 = image_features.astype(jnp.float32)
    power = lax.optimization_barrier(jnp.sum(feature_f32 * feature_f32, axis=0)) / D
    normed = raw_kv * lax.rsqrt(power + 1e-06)[:, None]
    slot_index = jnp.arange(total_slots, dtype=jnp.int32)
    shard_index = slot_index // slot_count
    within = slot_index % slot_count
    grid_rows = image_grids[shard_index]
    offsets = grid_rows[:, 0]
    grid_tall = grid_rows[:, 1]
    grid_wide = grid_rows[:, 2]
    live_slot = within < grid_tall * grid_wide
    image_start = shard_index * ROWS + offsets
    height_ids = image_start + within // grid_wide
    width_ids = image_start + within % grid_wide
    cosine, sine_table = rope_tables(image_start, height_ids, width_ids)
    key_heads = normed[:, :kv_width].reshape(total_slots, KV_HEADS, HEAD_DIM)
    image_keys = rotate(key_heads, cosine, sine_table).reshape(total_slots, kv_width).astype(jnp.bfloat16)
    image_values = normed[:, kv_width:].astype(jnp.bfloat16)
    length = ROWS * N_CTX
    places = jnp.where(live_slot, image_start + within, length).astype(jnp.int32)
    cache_keys = text_keys.at[places].set(image_keys, mode='drop')
    cache_values = text_values.at[places].set(image_values, mode='drop')
    attention = attend(queries, cache_keys, cache_values)
    return (attention, cache_keys, cache_values)
```

```python
import functools
import math

import jax
import jax.numpy as jnp
import numpy as np
from jax import lax
from jax.experimental import pallas as pl
from jax.experimental.pallas import tpu as pltpu
from jax.sharding import PartitionSpec as P

HEAD_DIM = 128
GRID = 4
SLOTS = GRID * GRID
BIG = 1 << 30
NEG = -1e30
F32 = jnp.float32
BF16 = jnp.bfloat16


def dot(x, y, cx, cy):
    return lax.dot_general(x, y, (((cx,), (cy,)), ((), ())), preferred_element_type=F32)


def kernel(
    n, inner,
    q_ref, tk_ref, tv_ref, feat_ref, w_ref, grid_ref, freq_ref,
    out_ref, ck_ref, cv_ref,
    tkv, img, meta, mine, p1_src, p1_dst, p2_src, p2_dst, qs, pos_t, pos_i, m_ref, acc_ref,
    meta_s, meta_r, p1_s, p1_r, p2_s, p2_r,
    tz_s, ty_s, t_r, tm_s, tm_r, i_s, i_r, im_s, im_r,
):
    chips = n // 2
    outer = chips // inner
    rows, width = tk_ref.shape
    kv = width // HEAD_DIM
    group = q_ref.shape[1] // width
    feats, slots = feat_ref.shape
    pair = 2 * SLOTS
    total_features = feats * n
    me = lax.axis_index("ctx")
    core = lax.rem(me, 2)
    chip = me // 2
    a = chip // inner
    b = lax.rem(chip, inner)
    mate = me + 1 - 2 * core

    def loop(low, high, f):
        lax.fori_loop(low, high, lambda i, c: (f(i), c)[1], 0)

    def copy(src, dst, send, recv, target):
        return pltpu.make_async_remote_copy(
            src_ref=src, dst_ref=dst, send_sem=send, recv_sem=recv,
            device_id={"ctx": target}, device_id_type=pl.DeviceIdType.MESH,
        )

    own = pl.ds(pl.multiple_of(me * rows, rows), rows)
    tkv[own, :width] = tk_ref[...]
    tkv[own, width:] = tv_ref[...]
    offset, tall, wide = grid_ref[0, 0], grid_ref[0, 1], grid_ref[0, 2]
    line = lax.broadcasted_iota(jnp.int32, (8, 128), 0)
    meta[me] = jnp.where(line == 0, offset, jnp.where(line == 1, tall, wide))
    img[...] = jnp.zeros_like(img)

    barrier = pltpu.get_barrier_semaphore()
    loop(1, n, lambda d: pl.semaphore_signal(
        barrier, inc=1, device_id={"ctx": lax.rem(me + d, n)},
        device_id_type=pl.DeviceIdType.MESH))
    pl.semaphore_wait(barrier, n - 1)

    def block(j):
        shard = 2 * j + core
        return tkv.at[pl.ds(pl.multiple_of(shard * rows, rows), rows), :]

    def meta_copy(d):
        return copy(meta.at[me], meta.at[me], meta_s.at[d], meta_r.at[me], lax.rem(me + d, n))

    def meta_in(j):
        return copy(meta.at[j], meta.at[j], meta_s.at[0], meta_r.at[j], mate)

    def up_copy(to):
        return copy(block(chip), block(chip), tz_s.at[to], t_r.at[chip],
                    2 * (to * inner + b) + core)

    def side_copy(from_a, d):
        j = from_a * inner + b
        return copy(block(j), block(j), ty_s.at[from_a * inner + d], t_r.at[j],
                    2 * (a * inner + lax.rem(b + d, inner)) + core)

    def t_in(j):
        return copy(block(j), block(j), tz_s.at[0], t_r.at[j], mate)

    def t_mate(j):
        return copy(block(j), block(j), tm_s.at[j], tm_r.at[j], mate)

    def t_mate_in(j):
        shard = 2 * j + 1 - core
        ref = tkv.at[pl.ds(pl.multiple_of(shard * rows, rows), rows), :]
        return copy(ref, ref, tm_s.at[j], tm_r.at[j], mate)

    loop(1, n, lambda d: meta_copy(d).start())

    half = lambda c: w_ref[:, pl.ds(pl.multiple_of(c * width, width), width)]
    features = feat_ref[...]
    p1_src[:, :width] = dot(features, half(1 - core), 0, 0).astype(BF16)
    wide_f = features.astype(F32)
    square = wide_f * wide_f
    high = square.astype(BF16)
    low = (square - high.astype(F32)).astype(BF16)
    ones = jnp.ones((feats, 128), BF16)
    power = dot(high, ones, 0, 0) + dot(low, ones, 0, 0)
    lane_s = lax.broadcasted_iota(jnp.int32, (slots, 128), 1)

    def split(x):
        top = x.astype(BF16)
        return jnp.where(lane_s < 64, top, (x - top.astype(F32)).astype(BF16))

    p1_src[:, width:] = split(power)
    p1 = copy(p1_src, p1_dst, p1_s, p1_r, mate)
    p1.start()
    mine[:, :width] = dot(features, half(core), 0, 0)
    mine[:, width:] = power
    p1.wait_recv()
    mine[:, :width] = mine[:, :width] + p1_dst[:, :width].astype(F32)
    other = p1_dst[:, width:].astype(F32)
    power = power + other[:, 0:1] + other[:, 64:65]
    mine[:, width:] = power
    p2_src[:, :width] = mine[:, :width].astype(BF16)
    p2_src[:, width:] = split(power)

    def p2_copy(d):
        j = lax.rem(chip + d, chips)
        return copy(p2_src.at[pl.ds(pl.multiple_of(j * pair, pair), pair), :], p2_dst.at[chip],
                    p2_s.at[d], p2_r.at[chip], 2 * j + core)

    def p2_in(j):
        return copy(p2_dst.at[j], p2_dst.at[j], p2_s.at[0], p2_r.at[j], mate)

    loop(1, chips, lambda d: p2_copy(d).start())
    loop(a + 1, outer, lambda to: up_copy(to).start())
    loop(1, inner, lambda d: side_copy(a, d).start())
    t_mate(chip).start()

    for g in range(kv):
        for h in range(group):
            at = (g * group + h) * HEAD_DIM
            qs[g, h * rows:(h + 1) * rows, :] = q_ref[:, at:at + HEAD_DIM]

    def meta_wait(d):
        meta_in(lax.rem(me + d, n)).wait_recv()

    loop(1, n, meta_wait)
    lane_t = lax.broadcasted_iota(jnp.int32, pos_t.shape, 1)
    lane_i = lax.broadcasted_iota(jnp.int32, pos_i.shape, 1)

    def place(j, carry):
        text, image = carry
        o, t, w = meta[j, 0:1, 0:1], meta[j, 1:2, 0:1], meta[j, 2:3, 0:1]
        begin = j * rows + o
        dead = (lane_t >= begin) & (lane_t < begin + t * w)
        k = lane_i - j * SLOTS
        live = (k >= 0) & (k < t * w)
        return jnp.where(dead, BIG, text), jnp.where(live, begin + k, image)

    text, image = lax.fori_loop(0, n, place, (lane_t, jnp.full(pos_i.shape, BIG, jnp.int32)))
    pos_t[...] = text
    pos_i[...] = image

    row = lax.broadcasted_iota(jnp.int32, (pair, 128), 0)
    lane = lax.broadcasted_iota(jnp.int32, (pair, 128), 1)
    second = row >= SLOTS
    k = jnp.where(second, row - SLOTS, row)
    pick = lambda i: jnp.where(second, meta[2 * chip + 1, i:i + 1, :], meta[2 * chip, i:i + 1, :])
    gw = pick(2)
    gy = jnp.zeros_like(k)
    for i in range(1, SLOTS // 2):
        gy = gy + jnp.where(k >= i * gw, 1, 0)
    gx = k - gy * gw
    t_id = (2 * chip + jnp.where(second, 1, 0)) * rows + pick(0)
    j = jnp.where(lane >= HEAD_DIM // 2, lane - HEAD_DIM // 2, lane)
    first_bound = HEAD_DIM // 8
    second_bound = first_bound + 3 * HEAD_DIM // 16
    ids = t_id + jnp.where(j < first_bound, 0, jnp.where(j < second_bound, gy, gx))
    angle = ids.astype(F32) * freq_ref[...]
    is_key = core == 0
    cosine = jnp.where(is_key, jnp.cos(angle), 1.0)
    sine = jnp.where(is_key, jnp.sin(angle), 0.0)
    sine = jnp.where(lane < HEAD_DIM // 2, -sine, sine)

    mine_rows = pl.ds(pl.multiple_of(chip * pair, pair), pair)

    def add(d, carry):
        total, extra = carry
        src = lax.rem(chip + d, chips)
        p2_in(src).wait_recv()
        return (total + p2_dst[src, :, :width].astype(F32),
                extra + p2_dst[src, :, width:].astype(F32))

    total, extra = lax.fori_loop(
        1, chips, add, (mine[mine_rows, :width], jnp.zeros((pair, 128), F32)))
    power = mine[mine_rows, width:] + extra[:, 0:1] + extra[:, 64:65]
    scale = lax.rsqrt(power / total_features + 1e-6)
    for h in range(kv):
        at = slice(h * HEAD_DIM, (h + 1) * HEAD_DIM)
        x = total[:, at] * scale
        turned = jnp.concatenate([x[:, HEAD_DIM // 2:], x[:, :HEAD_DIM // 2]], axis=1)
        img[core, chip, :, at] = (x * cosine + turned * sine).astype(BF16)

    def i_copy(j):
        return copy(img.at[core, chip], img.at[core, chip], i_s.at[j], i_r.at[chip], 2 * j + core)

    def i_in(j):
        return copy(img.at[core, j], img.at[core, j], i_s.at[0], i_r.at[j], mate)

    def i_mate(j):
        return copy(img.at[core, j], img.at[core, j], im_s.at[j], im_r.at[j], mate)

    def i_mate_in(j):
        return copy(img.at[1 - core, j], img.at[1 - core, j], im_s.at[j], im_r.at[j], mate)

    def others(low, high, f):
        def step(j):
            @pl.when(j != chip)
            def _():
                f(j)
        loop(low, high, step)

    seen = (a + 1) * inner
    others(a * inner, chips, lambda j: i_copy(j).start())
    i_mate(chip).start()

    def pass_on(i):
        from_a = a - 1 - i
        j = from_a * inner + b
        t_in(j).wait_recv()
        loop(1, inner, lambda d: side_copy(from_a, d).start())
        t_mate(j).start()

    loop(0, a, pass_on)

    def from_side(i):
        from_a = a - i

        def step(d):
            j = from_a * inner + lax.rem(b + d, inner)
            t_in(j).wait_recv()
            t_mate(j).start()

        loop(1, inner, step)

    loop(0, a + 1, from_side)

    def image_on(j):
        i_in(j).wait_recv()
        i_mate(j).start()

    others(0, seen, image_on)
    loop(0, seen, lambda j: t_mate_in(j).wait_recv())

    span = group * rows
    plane = 2 * inner * rows
    q_pos = me * rows + lax.rem(lax.broadcasted_iota(jnp.int32, (span, 1), 0), rows)
    factor = math.log2(math.e) / math.sqrt(HEAD_DIM)

    def attend(g, keys, values, pos):
        s = dot(qs[g], keys, 1, 1)
        s = jnp.where(pos <= q_pos, s, NEG)
        before = m_ref[g]
        now = jnp.maximum(before, jnp.max(s, axis=1, keepdims=True))
        shrink = jnp.exp2((before - now) * factor)
        weight = jnp.exp2((s - now[:, 0:1]) * factor).astype(BF16)
        both = jnp.concatenate([values, jnp.ones_like(values)], axis=1)
        product = dot(weight, both, 1, 0)
        acc_ref[g, :, :HEAD_DIM] = acc_ref[g, :, :HEAD_DIM] * shrink + product[:, :HEAD_DIM]
        acc_ref[g, :, HEAD_DIM:] = acc_ref[g, :, HEAD_DIM:] * shrink + product[:, HEAD_DIM:]
        m_ref[g] = now

    m_ref[...] = jnp.full(m_ref.shape, NEG, F32)
    acc_ref[...] = jnp.zeros_like(acc_ref)

    def text_step(p):
        at = pl.ds(pl.multiple_of(p * plane, plane), plane)
        pos = pos_t[:, at]
        for g in range(kv):
            lo = g * HEAD_DIM
            attend(g, tkv[at, lo:lo + HEAD_DIM], tkv[at, width + lo:width + lo + HEAD_DIM], pos)

    loop(0, a + 1, text_step)

    loop(0, seen, lambda j: i_mate_in(j).wait_recv())
    local = lax.broadcasted_iota(jnp.int32, (rows, SLOTS), 0)
    within = lax.broadcasted_iota(jnp.int32, (rows, SLOTS), 1)
    count = tall * wide
    hot = jnp.where((local == offset + within) & (within < count), 1.0, 0.0).astype(BF16)
    local = lax.broadcasted_iota(jnp.int32, (rows, width), 0)
    is_image = (local >= offset) & (local < offset + count)
    mine_slots = pl.ds(pl.multiple_of(core * SLOTS, SLOTS), SLOTS)
    for part, (ref, text_ref) in enumerate(((ck_ref, tk_ref), (cv_ref, tv_ref))):
        placed = dot(hot, img[part, chip, mine_slots, :], 1, 0)
        ref[...] = jnp.where(is_image, placed, text_ref[...].astype(F32)).astype(BF16)
    for g in range(kv):
        at = slice(g * HEAD_DIM, (g + 1) * HEAD_DIM)
        keys = img[0, :, :, at].reshape(slots, HEAD_DIM)
        values = img[1, :, :, at].reshape(slots, HEAD_DIM)
        attend(g, keys, values, pos_i[...])
        done = acc_ref[g, :, :HEAD_DIM] / acc_ref[g, :, HEAD_DIM:]
        for h in range(group):
            at = (g * group + h) * HEAD_DIM
            out_ref[:, at:at + HEAD_DIM] = done[h * rows:(h + 1) * rows].astype(BF16)

    loop(1, n, lambda d: meta_copy(d).wait_send())
    p1.wait_send()
    loop(1, chips, lambda d: p2_copy(d).wait_send())
    loop(a + 1, outer, lambda to: up_copy(to).wait_send())
    loop(0, a + 1, lambda f: loop(1, inner, lambda d: side_copy(f, d).wait_send()))
    loop(0, seen, lambda j: t_mate(j).wait_send())
    others(a * inner, chips, lambda j: i_copy(j).wait_send())
    loop(0, seen, lambda j: i_mate(j).wait_send())


def body(n, queries, text_keys, text_values, image_features, kv_weight, image_grids):
    chips = n // 2
    inner = 1
    while (2 * inner) ** 2 <= chips and chips % (2 * inner) == 0:
        inner *= 2
    outer = chips // inner
    rows, width = text_keys.shape
    kv = width // HEAD_DIM
    span = queries.shape[1] // width * rows
    slots = image_features.shape[1]
    pair = 2 * SLOTS
    j = np.arange(HEAD_DIM, dtype=np.float64) % (HEAD_DIM // 2)
    freq = jnp.asarray((1000000.0 ** (-2.0 * j / HEAD_DIM)).astype(np.float32)[None, :])
    dma = pltpu.SemaphoreType.DMA
    vmem = pl.BlockSpec(memory_space=pltpu.VMEM)
    smem = pl.BlockSpec(memory_space=pltpu.SMEM)
    return pl.pallas_call(
        functools.partial(kernel, n, inner),
        out_shape=(
            jax.ShapeDtypeStruct(queries.shape, BF16),
            jax.ShapeDtypeStruct(text_keys.shape, BF16),
            jax.ShapeDtypeStruct(text_values.shape, BF16),
        ),
        in_specs=[vmem] * 5 + [smem, vmem],
        out_specs=(vmem,) * 3,
        scratch_shapes=[
            pltpu.VMEM((n * rows, 2 * width), BF16),
            pltpu.VMEM((2, chips, pair, width), BF16),
            pltpu.VMEM((n, 8, 128), jnp.int32),
            pltpu.VMEM((slots, width + 128), F32),
            pltpu.VMEM((slots, width + 128), BF16),
            pltpu.VMEM((slots, width + 128), BF16),
            pltpu.VMEM((slots, width + 128), BF16),
            pltpu.VMEM((chips, pair, width + 128), BF16),
            pltpu.VMEM((kv, span, HEAD_DIM), BF16),
            pltpu.VMEM((1, n * rows), jnp.int32),
            pltpu.VMEM((1, slots), jnp.int32),
            pltpu.VMEM((kv, span, HEAD_DIM), F32),
            pltpu.VMEM((kv, span, 2 * HEAD_DIM), F32),
            dma((n,)), dma((n,)), dma, dma, dma((chips,)), dma((chips,)),
            dma((outer,)), dma((chips,)), dma((chips,)), dma((chips,)), dma((chips,)),
            dma((chips,)), dma((chips,)), dma((chips,)), dma((chips,)),
        ],
        compiler_params=pltpu.CompilerParams(
            collective_id=0, has_side_effects=True, vmem_limit_bytes=60 * 1024 * 1024
        ),
        cost_estimate=pl.CostEstimate(
            flops=4 * n * rows * queries.size, bytes_accessed=4 * queries.size,
            transcendentals=n * rows * rows * 32),
    )(queries, text_keys, text_values, image_features, kv_weight, image_grids, freq)


def solution(mesh):
    both = P(("groups", "ctx"), None)
    return jax.shard_map(
        functools.partial(body, mesh.shape["ctx"]), mesh=mesh,
        in_specs=(both, both, both, both, P("ctx", None), both),
        out_specs=(both, both, both), check_vma=False)
```

```python
import functools
import math

import jax
import jax.numpy as jnp
import numpy as np
from jax import lax
from jax.experimental import pallas as pl
from jax.experimental.pallas import tpu as pltpu
from jax.sharding import PartitionSpec as P

HEAD_DIM = 128
GRID = 4
SLOTS = GRID * GRID
BIG = 1 << 30
NEG = -1e30
F32 = jnp.float32
BF16 = jnp.bfloat16


def dot(x, y, cx, cy):
    return lax.dot_general(x, y, (((cx,), (cy,)), ((), ())), preferred_element_type=F32)


def kernel(
    n, inner,
    q_ref, tk_ref, tv_ref, feat_ref, w_ref, grid_ref, freq_ref,
    out_ref, ck_ref, cv_ref,
    tkv, img, meta, mine, p1_src, p1_dst, p2_src, p2_dst, qs, pos_t, pos_i, m_ref, acc_ref,
    meta_s, meta_r, p1_s, p1_r, p2_s, p2_r,
    tz_s, ty_s, t_r, tm_s, tm_r, i_s, i_r, im_s, im_r,
):
    chips = n // 2
    outer = chips // inner
    rows, width = tk_ref.shape
    kv = width // HEAD_DIM
    group = q_ref.shape[1] // width
    feats, slots = feat_ref.shape
    pair = 2 * SLOTS
    total_features = feats * n
    me = lax.axis_index("ctx")
    core = lax.rem(me, 2)
    chip = me // 2
    a = chip // inner
    b = lax.rem(chip, inner)
    mate = me + 1 - 2 * core

    def loop(low, high, f):
        lax.fori_loop(low, high, lambda i, c: (f(i), c)[1], 0)

    def copy(src, dst, send, recv, target):
        return pltpu.make_async_remote_copy(
            src_ref=src, dst_ref=dst, send_sem=send, recv_sem=recv,
            device_id={"ctx": target}, device_id_type=pl.DeviceIdType.MESH,
        )

    own = pl.ds(pl.multiple_of(me * rows, rows), rows)
    tkv[:, width:] = jnp.zeros((n * rows, width), BF16)
    tkv[own, :width] = tk_ref[...]
    tkv[own, width:] = tv_ref[...]
    offset, tall, wide = grid_ref[0, 0], grid_ref[0, 1], grid_ref[0, 2]
    line = lax.broadcasted_iota(jnp.int32, (8, 128), 0)
    meta[me] = jnp.where(line == 0, offset, jnp.where(line == 1, tall, wide))
    img[...] = jnp.zeros_like(img)

    barrier = pltpu.get_barrier_semaphore()
    loop(1, n, lambda d: pl.semaphore_signal(
        barrier, inc=1, device_id={"ctx": lax.rem(me + d, n)},
        device_id_type=pl.DeviceIdType.MESH))
    pl.semaphore_wait(barrier, n - 1)

    def block(j):
        shard = 2 * j + core
        return tkv.at[pl.ds(pl.multiple_of(shard * rows, rows), rows), :]

    def meta_copy(d):
        return copy(meta.at[me], meta.at[me], meta_s.at[d], meta_r.at[me], lax.rem(me + d, n))

    def meta_in(j):
        return copy(meta.at[j], meta.at[j], meta_s.at[0], meta_r.at[j], mate)

    def up_copy(to):
        return copy(block(chip), block(chip), tz_s.at[to], t_r.at[chip],
                    2 * (to * inner + b) + core)

    def side_copy(from_a, d):
        j = from_a * inner + b
        return copy(block(j), block(j), ty_s.at[from_a * inner + d], t_r.at[j],
                    2 * (a * inner + lax.rem(b + d, inner)) + core)

    def t_in(j):
        return copy(block(j), block(j), tz_s.at[0], t_r.at[j], mate)

    def t_mate(j):
        return copy(block(j), block(j), tm_s.at[j], tm_r.at[j], mate)

    def t_mate_in(j):
        shard = 2 * j + 1 - core
        ref = tkv.at[pl.ds(pl.multiple_of(shard * rows, rows), rows), :]
        return copy(ref, ref, tm_s.at[j], tm_r.at[j], mate)

    loop(1, n, lambda d: meta_copy(d).start())
    loop(a + 1, outer, lambda to: up_copy(to).start())
    loop(1, inner, lambda d: side_copy(a, d).start())

    half = lambda c: w_ref[:, pl.ds(pl.multiple_of(c * width, width), width)]
    features = feat_ref[...].T
    p1_src[:, :width] = dot(features, half(1 - core), 1, 0).astype(BF16)
    wide_f = features.astype(F32)
    power = jnp.sum(wide_f * wide_f, axis=1, keepdims=True)
    power = jnp.broadcast_to(power, (slots, 128))
    lane_s = lax.broadcasted_iota(jnp.int32, (slots, 128), 1)

    def split(x):
        top = x.astype(BF16)
        return jnp.where(lane_s < 64, top, (x - top.astype(F32)).astype(BF16))

    p1_src[:, width:] = split(power)
    p1 = copy(p1_src, p1_dst, p1_s, p1_r, mate)
    p1.start()
    mine[:, :width] = dot(features, half(core), 1, 0)
    mine[:, width:] = power
    p1.wait_recv()
    mine[:, :width] = mine[:, :width] + p1_dst[:, :width].astype(F32)
    other = p1_dst[:, width:].astype(F32)
    power = power + other[:, 0:1] + other[:, 64:65]
    mine[:, width:] = power
    p2_src[:, :width] = mine[:, :width].astype(BF16)
    p2_src[:, width:] = split(power)

    def p2_copy(d):
        j = lax.rem(chip + d, chips)
        return copy(p2_src.at[pl.ds(pl.multiple_of(j * pair, pair), pair), :], p2_dst.at[chip],
                    p2_s.at[d], p2_r.at[chip], 2 * j + core)

    def p2_in(j):
        return copy(p2_dst.at[j], p2_dst.at[j], p2_s.at[0], p2_r.at[j], mate)

    loop(1, chips, lambda d: p2_copy(d).start())
    t_mate(chip).start()

    for g in range(kv):
        for h in range(group):
            at = (g * group + h) * HEAD_DIM
            qs[g, h * rows:(h + 1) * rows, :] = q_ref[:, at:at + HEAD_DIM]

    def meta_wait(d):
        meta_in(lax.rem(me + d, n)).wait_recv()

    loop(1, n, meta_wait)
    lane_t = lax.broadcasted_iota(jnp.int32, pos_t.shape, 1)
    lane_i = lax.broadcasted_iota(jnp.int32, pos_i.shape, 1)

    def place(j, carry):
        text, image = carry
        o, t, w = meta[j, 0:1, 0:1], meta[j, 1:2, 0:1], meta[j, 2:3, 0:1]
        begin = j * rows + o
        dead = (lane_t >= begin) & (lane_t < begin + t * w)
        k = lane_i - j * SLOTS
        live = (k >= 0) & (k < t * w)
        return jnp.where(dead, BIG, text), jnp.where(live, begin + k, image)

    text, image = lax.fori_loop(0, n, place, (lane_t, jnp.full(pos_i.shape, BIG, jnp.int32)))
    pos_t[...] = text
    pos_i[...] = image

    row = lax.broadcasted_iota(jnp.int32, (pair, 128), 0)
    lane = lax.broadcasted_iota(jnp.int32, (pair, 128), 1)
    second = row >= SLOTS
    k = jnp.where(second, row - SLOTS, row)
    pick = lambda i: jnp.where(second, meta[2 * chip + 1, i:i + 1, :], meta[2 * chip, i:i + 1, :])
    gw = pick(2)
    gy = jnp.zeros_like(k)
    for i in range(1, SLOTS // 2):
        gy = gy + jnp.where(k >= i * gw, 1, 0)
    gx = k - gy * gw
    t_id = (2 * chip + jnp.where(second, 1, 0)) * rows + pick(0)
    j = jnp.where(lane >= HEAD_DIM // 2, lane - HEAD_DIM // 2, lane)
    first_bound = HEAD_DIM // 8
    second_bound = first_bound + 3 * HEAD_DIM // 16
    ids = t_id + jnp.where(j < first_bound, 0, jnp.where(j < second_bound, gy, gx))
    angle = ids.astype(F32) * freq_ref[...]
    is_key = core == 0
    cosine = jnp.where(is_key, jnp.cos(angle), 1.0)
    sine = jnp.where(is_key, jnp.sin(angle), 0.0)
    sine = jnp.where(lane < HEAD_DIM // 2, -sine, sine)

    def pass_on(i):
        from_a = a - 1 - i
        j = from_a * inner + b
        t_in(j).wait_recv()
        loop(1, inner, lambda d: side_copy(from_a, d).start())
        t_mate(j).start()

    loop(0, a, pass_on)

    mine_rows = pl.ds(pl.multiple_of(chip * pair, pair), pair)

    def add(d, carry):
        total, extra = carry
        src = lax.rem(chip + d, chips)
        p2_in(src).wait_recv()
        return (total + p2_dst[src, :, :width].astype(F32),
                extra + p2_dst[src, :, width:].astype(F32))

    total, extra = lax.fori_loop(
        1, chips, add, (mine[mine_rows, :width], jnp.zeros((pair, 128), F32)))
    power = mine[mine_rows, width:] + extra[:, 0:1] + extra[:, 64:65]
    scale = lax.rsqrt(power / total_features + 1e-6)
    for h in range(kv):
        at = slice(h * HEAD_DIM, (h + 1) * HEAD_DIM)
        x = total[:, at] * scale
        turned = jnp.concatenate([x[:, HEAD_DIM // 2:], x[:, :HEAD_DIM // 2]], axis=1)
        img[core, chip, :, at] = (x * cosine + turned * sine).astype(BF16)

    def i_copy(j):
        return copy(img.at[core, chip], img.at[core, chip], i_s.at[j], i_r.at[chip], 2 * j + core)

    def i_in(j):
        return copy(img.at[core, j], img.at[core, j], i_s.at[0], i_r.at[j], mate)

    def i_mate(j):
        return copy(img.at[core, j], img.at[core, j], im_s.at[j], im_r.at[j], mate)

    def i_mate_in(j):
        return copy(img.at[1 - core, j], img.at[1 - core, j], im_s.at[j], im_r.at[j], mate)

    def others(low, high, f):
        def step(j):
            @pl.when(j != chip)
            def _():
                f(j)
        loop(low, high, step)

    seen = (a + 1) * inner
    others(a * inner, chips, lambda j: i_copy(j).start())
    i_mate(chip).start()

    def from_side(i):
        from_a = a - i

        def step(d):
            j = from_a * inner + lax.rem(b + d, inner)
            t_in(j).wait_recv()
            t_mate(j).start()

        loop(1, inner, step)

    loop(0, a + 1, from_side)

    loop(0, seen, lambda j: t_mate_in(j).wait_recv())

    span = group * rows
    part = math.gcd(span, 256)
    block_keys = math.gcd(n * rows, 1024)
    key_blocks = n * rows // block_keys
    factor = math.log2(math.e) / math.sqrt(HEAD_DIM)
    q_pos = me * rows + lax.rem(lax.broadcasted_iota(jnp.int32, (part, 1), 0), rows)

    def attend(g, r, keys, values, pos, first):
        at = slice(r * part, (r + 1) * part)
        s = dot(qs[g, at, :], keys, 1, 1)
        s = jnp.where(pos <= q_pos, s, NEG)
        now = jnp.broadcast_to(jnp.max(s, axis=1, keepdims=True), (part, HEAD_DIM))
        if not first:
            before = m_ref[g, at, :]
            now = jnp.maximum(before, now)
        shift = jnp.concatenate([now] * (s.shape[1] // HEAD_DIM), axis=1)
        weight = jnp.exp2((s - shift) * factor).astype(BF16)
        both = jnp.concatenate([values, jnp.ones_like(values)], axis=1)
        product = dot(weight, both, 1, 0)
        summed, totals = product[:, :HEAD_DIM], product[:, HEAD_DIM:]
        if not first:
            shrink = jnp.exp2((before - now) * factor)
            summed = summed + acc_ref[g, at, :HEAD_DIM] * shrink
            totals = totals + acc_ref[g, at, HEAD_DIM:] * shrink
        return now, summed, totals

    def text_block(g, r, p, first):
        at = pl.ds(pl.multiple_of(p * block_keys, block_keys), block_keys)
        lo = g * HEAD_DIM
        now, summed, totals = attend(
            g, r, tkv[at, lo:lo + HEAD_DIM], tkv[at, width + lo:width + lo + HEAD_DIM],
            pos_t[:, at], first)
        at = slice(r * part, (r + 1) * part)
        m_ref[g, at, :] = now
        acc_ref[g, at, :HEAD_DIM] = summed
        acc_ref[g, at, HEAD_DIM:] = totals

    def text_heads(heads):
        for g in heads:
            for r in range(span // part):
                text_block(g, r, 0, True)
        if key_blocks > 1:
            def more(p):
                for g in heads:
                    for r in range(span // part):
                        text_block(g, r, p, False)
            loop(1, (me * rows + rows - 1) // block_keys + 1, more)

    def image_on(j):
        i_in(j).wait_recv()
        i_mate(j).start()

    text_heads(range(kv // 2))
    others(0, seen, image_on)
    text_heads(range(kv // 2, kv))

    loop(0, seen, lambda j: i_mate_in(j).wait_recv())
    local = lax.broadcasted_iota(jnp.int32, (rows, SLOTS), 0)
    within = lax.broadcasted_iota(jnp.int32, (rows, SLOTS), 1)
    count = tall * wide
    hot = jnp.where((local == offset + within) & (within < count), 1.0, 0.0).astype(BF16)
    local = lax.broadcasted_iota(jnp.int32, (rows, width), 0)
    is_image = (local >= offset) & (local < offset + count)
    mine_slots = pl.ds(pl.multiple_of(core * SLOTS, SLOTS), SLOTS)
    for c, (ref, text_ref) in enumerate(((ck_ref, tk_ref), (cv_ref, tv_ref))):
        placed = dot(hot, img[c, chip, mine_slots, :], 1, 0)
        ref[...] = jnp.where(is_image, placed, text_ref[...].astype(F32)).astype(BF16)
    for g in range(kv):
        lanes = slice(g * HEAD_DIM, (g + 1) * HEAD_DIM)
        keys = img[0, :, :, lanes].reshape(slots, HEAD_DIM)
        values = img[1, :, :, lanes].reshape(slots, HEAD_DIM)
        for r in range(span // part):
            now, summed, totals = attend(g, r, keys, values, pos_i[...], False)
            done = (summed / totals).astype(BF16)
            for h in range(part // rows):
                at = (g * group + r * (part // rows) + h) * HEAD_DIM
                out_ref[:, at:at + HEAD_DIM] = done[h * rows:(h + 1) * rows]

    loop(1, n, lambda d: meta_copy(d).wait_send())
    p1.wait_send()
    loop(1, chips, lambda d: p2_copy(d).wait_send())
    loop(a + 1, outer, lambda to: up_copy(to).wait_send())
    loop(0, a + 1, lambda f: loop(1, inner, lambda d: side_copy(f, d).wait_send()))
    loop(0, seen, lambda j: t_mate(j).wait_send())
    others(a * inner, chips, lambda j: i_copy(j).wait_send())
    loop(0, seen, lambda j: i_mate(j).wait_send())


def body(n, queries, text_keys, text_values, image_features, kv_weight, image_grids):
    chips = n // 2
    inner = 1
    while (2 * inner) ** 2 <= chips and chips % (2 * inner) == 0:
        inner *= 2
    outer = chips // inner
    rows, width = text_keys.shape
    kv = width // HEAD_DIM
    span = queries.shape[1] // width * rows
    slots = image_features.shape[1]
    pair = 2 * SLOTS
    j = np.arange(HEAD_DIM, dtype=np.float64) % (HEAD_DIM // 2)
    freq = jnp.asarray((1000000.0 ** (-2.0 * j / HEAD_DIM)).astype(np.float32)[None, :])
    dma = pltpu.SemaphoreType.DMA
    vmem = pl.BlockSpec(memory_space=pltpu.VMEM)
    smem = pl.BlockSpec(memory_space=pltpu.SMEM)
    return pl.pallas_call(
        functools.partial(kernel, n, inner),
        out_shape=(
            jax.ShapeDtypeStruct(queries.shape, BF16),
            jax.ShapeDtypeStruct(text_keys.shape, BF16),
            jax.ShapeDtypeStruct(text_values.shape, BF16),
        ),
        in_specs=[vmem] * 5 + [smem, vmem],
        out_specs=(vmem,) * 3,
        scratch_shapes=[
            pltpu.VMEM((n * rows, 2 * width), BF16),
            pltpu.VMEM((2, chips, pair, width), BF16),
            pltpu.VMEM((n, 8, 128), jnp.int32),
            pltpu.VMEM((slots, width + 128), F32),
            pltpu.VMEM((slots, width + 128), BF16),
            pltpu.VMEM((slots, width + 128), BF16),
            pltpu.VMEM((slots, width + 128), BF16),
            pltpu.VMEM((chips, pair, width + 128), BF16),
            pltpu.VMEM((kv, span, HEAD_DIM), BF16),
            pltpu.VMEM((1, n * rows), jnp.int32),
            pltpu.VMEM((1, slots), jnp.int32),
            pltpu.VMEM((kv, span, HEAD_DIM), F32),
            pltpu.VMEM((kv, span, 2 * HEAD_DIM), F32),
            dma((n,)), dma((n,)), dma, dma, dma((chips,)), dma((chips,)),
            dma((outer,)), dma((chips,)), dma((chips,)), dma((chips,)), dma((chips,)),
            dma((chips,)), dma((chips,)), dma((chips,)), dma((chips,)),
        ],
        compiler_params=pltpu.CompilerParams(
            collective_id=0, has_side_effects=True, vmem_limit_bytes=60 * 1024 * 1024
        ),
        cost_estimate=pl.CostEstimate(
            flops=4 * n * rows * queries.size, bytes_accessed=4 * queries.size,
            transcendentals=n * rows * rows * 32),
    )(queries, text_keys, text_values, image_features, kv_weight, image_grids, freq)


def solution(mesh):
    both = P(("groups", "ctx"), None)
    return jax.shard_map(
        functools.partial(body, mesh.shape["ctx"]), mesh=mesh,
        in_specs=(both, both, both, both, P("ctx", None), both),
        out_specs=(both, both, both), check_vma=False)
```

```python
import functools
import math

import jax
import jax.numpy as jnp
import numpy as np
from jax import lax
from jax.experimental import pallas as pl
from jax.experimental.pallas import tpu as pltpu
from jax.sharding import PartitionSpec as P

HEAD_DIM = 128
GRID = 4
SLOTS = GRID * GRID
BIG = 1 << 30
NEG = -1e30
F32 = jnp.float32
BF16 = jnp.bfloat16


def dot(x, y, cx, cy):
    return lax.dot_general(x, y, (((cx,), (cy,)), ((), ())), preferred_element_type=F32)


def kernel(
    n, inner,
    q_hbm, tk_ref, tv_ref, feat_hbm, w_hbm, grid_ref, freq_ref,
    out_ref, ck_ref, cv_ref,
    q_ref, feat_ref, w_ref, load_s, tkv, img, info, info_sum, mine, p1_src, p1_dst, p2_src, p2_dst, qs, pos_t, pos_i, m_ref, acc_ref,
    info_s, info_r, p1_s, p1_r, p2_s, p2_r,
    tz_s, ty_s, t_r, tm_s, tm_r, i_s, is_s, i_r, im_s, im_r,
):
    chips = n // 2
    outer = chips // inner
    rows, width = tk_ref.shape
    kv = width // HEAD_DIM
    group = q_ref.shape[1] // width
    feats, slots = feat_ref.shape
    pair = 2 * SLOTS
    total_features = feats * n
    me = lax.axis_index("ctx")
    core = lax.rem(me, 2)
    chip = me // 2
    a = chip // inner
    b = lax.rem(chip, inner)
    mate = me + 1 - 2 * core

    def loop(low, high, f):
        lax.fori_loop(low, high, lambda i, c: (f(i), c)[1], 0)

    def copy(src, dst, send, recv, target):
        return pltpu.make_async_remote_copy(
            src_ref=src, dst_ref=dst, send_sem=send, recv_sem=recv,
            device_id={"ctx": target}, device_id_type=pl.DeviceIdType.MESH,
        )

    loads = [pltpu.make_async_copy(src, dst, load_s.at[i]) for i, (src, dst) in enumerate(
        ((feat_hbm, feat_ref), (w_hbm, w_ref), (q_hbm, q_ref)))]
    for load in loads:
        load.start()

    own = pl.ds(pl.multiple_of(me * rows, rows), rows)
    tkv[:, width:] = jnp.zeros((n * rows, width), BF16)
    tkv[own, :width] = tk_ref[...]
    tkv[own, width:] = tv_ref[...]
    offset, tall, wide = grid_ref[0, 0], grid_ref[0, 1], grid_ref[0, 2]
    img[...] = jnp.zeros_like(img)

    barrier = pltpu.get_barrier_semaphore()
    loop(1, n, lambda d: pl.semaphore_signal(
        barrier, inc=1, device_id={"ctx": lax.rem(me + d, n)},
        device_id_type=pl.DeviceIdType.MESH))
    pl.semaphore_wait(barrier, n - 1)

    def block(j):
        shard = 2 * j + core
        return tkv.at[pl.ds(pl.multiple_of(shard * rows, rows), rows), :]

    def info_copy(d):
        return copy(info.at[me], info.at[me], info_s.at[d], info_r.at[me], lax.rem(me + d, n))

    def info_in(j):
        return copy(info.at[j], info.at[j], info_s.at[0], info_r.at[j], mate)

    def up_copy(from_a):
        j = from_a * inner + b
        return copy(block(j), block(j), tz_s.at[from_a], t_r.at[j], me + 2 * inner)

    def side_copy(from_a, d):
        j = from_a * inner + b
        return copy(block(j), block(j), ty_s.at[from_a * inner + d], t_r.at[j],
                    2 * (a * inner + lax.rem(b + d, inner)) + core)

    def t_in(j):
        return copy(block(j), block(j), tz_s.at[0], t_r.at[j], mate)

    def t_mate(j):
        return copy(block(j), block(j), tm_s.at[j], tm_r.at[j], mate)

    def t_mate_in(j):
        shard = 2 * j + 1 - core
        ref = tkv.at[pl.ds(pl.multiple_of(shard * rows, rows), rows), :]
        return copy(ref, ref, tm_s.at[j], tm_r.at[j], mate)

    @pl.when(a + 1 < outer)
    def _():
        up_copy(a).start()

    loop(1, inner, lambda d: side_copy(a, d).start())
    t_mate(chip).start()

    loads[0].wait()
    wide_f = feat_ref[...].astype(F32)
    power = jnp.sum(wide_f * wide_f, axis=0, keepdims=True)
    line = lax.broadcasted_iota(jnp.int32, info.shape[1:], 0)
    facts = jnp.where(line == 0, offset, jnp.where(line == 1, tall, wide)).astype(F32)
    for i in range(slots // 128):
        facts = jnp.where(line == 3 + i, power[:, i * 128:(i + 1) * 128], facts)
    info[me] = facts
    loop(1, n, lambda d: info_copy(d).start())

    half = lambda c: w_ref[:, pl.ds(pl.multiple_of(c * width, width), width)]
    features = feat_ref[...].T
    loads[1].wait()
    p1_src[...] = dot(features, half(1 - core), 1, 0).astype(BF16)
    p1 = copy(p1_src, p1_dst, p1_s, p1_r, mate)
    p1.start()
    mine[...] = dot(features, half(core), 1, 0)
    p1.wait_recv()
    both_cores = mine[...] + p1_dst[...].astype(F32)
    mine[...] = both_cores
    p2_src[...] = both_cores.astype(BF16)

    def p2_copy(d):
        j = lax.rem(chip + d, chips)
        return copy(p2_src.at[pl.ds(pl.multiple_of(j * pair, pair), pair), :], p2_dst.at[chip],
                    p2_s.at[d], p2_r.at[chip], 2 * j + core)

    def p2_in(j):
        return copy(p2_dst.at[j], p2_dst.at[j], p2_s.at[0], p2_r.at[j], mate)

    loop(1, chips, lambda d: p2_copy(d).start())

    def pass_on(i):
        from_a = a - 1 - i
        j = from_a * inner + b
        t_in(j).wait_recv()

        @pl.when(a + 1 < outer)
        def _():
            up_copy(from_a).start()

        loop(1, inner, lambda d: side_copy(from_a, d).start())
        t_mate(j).start()

    early = jnp.minimum(a, 2)
    loop(0, jnp.minimum(a, 1), pass_on)

    loads[2].wait()
    for g in range(kv):
        for h in range(group):
            at = (g * group + h) * HEAD_DIM
            qs[g, h * rows:(h + 1) * rows, :] = q_ref[:, at:at + HEAD_DIM]

    def gather_facts(d, total):
        j = lax.rem(me + d, n)
        info_in(j).wait_recv()
        return total + info[j]

    info_sum[...] = lax.fori_loop(1, n, gather_facts, info[me])

    row = lax.broadcasted_iota(jnp.int32, (pair, 128), 0)
    lane = lax.broadcasted_iota(jnp.int32, (pair, 128), 1)
    second = row >= SLOTS
    k = jnp.where(second, row - SLOTS, row)
    pick = lambda i: jnp.where(
        second, info[2 * chip + 1, i:i + 1, :], info[2 * chip, i:i + 1, :]).astype(jnp.int32)
    gw = pick(2)
    gy = jnp.zeros_like(k)
    for i in range(1, SLOTS // 2):
        gy = gy + jnp.where(k >= i * gw, 1, 0)
    gx = k - gy * gw
    t_id = (2 * chip + jnp.where(second, 1, 0)) * rows + pick(0)
    j = jnp.where(lane >= HEAD_DIM // 2, lane - HEAD_DIM // 2, lane)
    first_bound = HEAD_DIM // 8
    second_bound = first_bound + 3 * HEAD_DIM // 16
    ids = t_id + jnp.where(j < first_bound, 0, jnp.where(j < second_bound, gy, gx))
    angle = ids.astype(F32) * freq_ref[...]
    is_key = core == 0
    cosine = jnp.where(is_key, jnp.cos(angle), 1.0)
    sine = jnp.where(is_key, jnp.sin(angle), 0.0)
    sine = jnp.where(lane < HEAD_DIM // 2, -sine, sine)

    loop(jnp.minimum(a, 1), early, pass_on)

    mine_rows = pl.ds(pl.multiple_of(chip * pair, pair), pair)

    def add(d, total):
        src = lax.rem(chip + d, chips)
        p2_in(src).wait_recv()
        return total + p2_dst[src].astype(F32)

    total = lax.fori_loop(1, chips, add, mine[mine_rows, :])
    squares = info_sum[pl.ds(3 + chip * pair // 128, 1), :]
    squares = jnp.where(lane == lax.rem(chip * pair, 128) + row, squares, 0.0)
    power = jnp.sum(squares, axis=1, keepdims=True)
    scale = lax.rsqrt(power / total_features + 1e-6)
    for h in range(kv):
        at = slice(h * HEAD_DIM, (h + 1) * HEAD_DIM)
        x = total[:, at] * scale
        turned = jnp.concatenate([x[:, HEAD_DIM // 2:], x[:, :HEAD_DIM // 2]], axis=1)
        img[core, chip, :, at] = (x * cosine + turned * sine).astype(BF16)

    def i_copy(to_a):
        return copy(img.at[core, chip], img.at[core, chip], i_s.at[to_a], i_r.at[chip],
                    2 * (to_a * inner + b) + core)

    def i_side(from_a, d):
        j = from_a * inner + b
        return copy(img.at[core, j], img.at[core, j], is_s.at[from_a * inner + d], i_r.at[j],
                    2 * (a * inner + lax.rem(b + d, inner)) + core)

    def i_in(j):
        return copy(img.at[core, j], img.at[core, j], i_s.at[0], i_r.at[j], mate)

    def i_mate(j):
        return copy(img.at[core, j], img.at[core, j], im_s.at[j], im_r.at[j], mate)

    def i_mate_in(j):
        return copy(img.at[1 - core, j], img.at[1 - core, j], im_s.at[j], im_r.at[j], mate)

    seen = (a + 1) * inner
    loop(a + 1, outer, lambda to: i_copy(to).start())
    loop(1, inner, lambda d: i_side(a, d).start())
    i_mate(chip).start()
    loop(early, a, pass_on)

    def from_side(i):
        from_a = a - i

        def step(d):
            j = from_a * inner + lax.rem(b + d, inner)
            t_in(j).wait_recv()
            t_mate(j).start()

        loop(1, inner, step)

    loop(0, a + 1, from_side)

    lane_t = lax.broadcasted_iota(jnp.int32, pos_t.shape, 1)
    lane_i = lax.broadcasted_iota(jnp.int32, pos_i.shape, 1)

    def place(j, carry):
        text, image = carry
        o, t, w = (info[j, i:i + 1, 0:1].astype(jnp.int32) for i in range(3))
        begin = j * rows + o
        dead = (lane_t >= begin) & (lane_t < begin + t * w)
        k = lane_i - j * SLOTS
        live = (k >= 0) & (k < t * w)
        return jnp.where(dead, BIG, text), jnp.where(live, begin + k, image)

    text, image = lax.fori_loop(0, n, place, (lane_t, jnp.full(pos_i.shape, BIG, jnp.int32)))
    pos_t[...] = text
    pos_i[...] = image

    loop(0, seen, lambda j: t_mate_in(j).wait_recv())

    span = group * rows
    part = math.gcd(span, 256)
    block_keys = math.gcd(n * rows, 1024)
    key_blocks = n * rows // block_keys
    factor = math.log2(math.e) / math.sqrt(HEAD_DIM)
    q_pos = me * rows + lax.rem(lax.broadcasted_iota(jnp.int32, (part, 1), 0), rows)

    def attend(g, r, keys, values, pos, first):
        at = slice(r * part, (r + 1) * part)
        s = dot(qs[g, at, :], keys, 1, 1)
        s = jnp.where(pos <= q_pos, s, NEG)
        now = jnp.broadcast_to(jnp.max(s, axis=1, keepdims=True), (part, HEAD_DIM))
        if not first:
            before = m_ref[g, at, :]
            now = jnp.maximum(before, now)
        shift = jnp.concatenate([now] * (s.shape[1] // HEAD_DIM), axis=1)
        weight = jnp.exp2((s - shift) * factor).astype(BF16)
        both = jnp.concatenate([values, jnp.ones_like(values)], axis=1)
        product = dot(weight, both, 1, 0)
        summed, totals = product[:, :HEAD_DIM], product[:, HEAD_DIM:]
        if not first:
            shrink = jnp.exp2((before - now) * factor)
            summed = summed + acc_ref[g, at, :HEAD_DIM] * shrink
            totals = totals + acc_ref[g, at, HEAD_DIM:] * shrink
        return now, summed, totals

    def text_block(g, r, p, first):
        at = pl.ds(pl.multiple_of(p * block_keys, block_keys), block_keys)
        lo = g * HEAD_DIM
        now, summed, totals = attend(
            g, r, tkv[at, lo:lo + HEAD_DIM], tkv[at, width + lo:width + lo + HEAD_DIM],
            pos_t[:, at], first)
        at = slice(r * part, (r + 1) * part)
        m_ref[g, at, :] = now
        acc_ref[g, at, :HEAD_DIM] = summed
        acc_ref[g, at, HEAD_DIM:] = totals

    def text_heads(heads):
        for g in heads:
            for r in range(span // part):
                text_block(g, r, 0, True)
        if key_blocks > 1:
            def more(p):
                for g in heads:
                    for r in range(span // part):
                        text_block(g, r, p, False)
            loop(1, (me * rows + rows - 1) // block_keys + 1, more)

    def image_on(from_a):
        j = from_a * inner + b
        i_in(j).wait_recv()
        loop(1, inner, lambda d: i_side(from_a, d).start())
        i_mate(j).start()

    def image_from_side(from_a):
        def step(d):
            j = from_a * inner + lax.rem(b + d, inner)
            i_in(j).wait_recv()
            i_mate(j).start()

        loop(1, inner, step)

    text_heads(range(kv - 2))
    loop(0, a, image_on)
    text_heads(range(kv - 2, kv - 1))
    loop(0, a + 1, image_from_side)
    text_heads(range(kv - 1, kv))

    loop(0, seen, lambda j: i_mate_in(j).wait_recv())
    local = lax.broadcasted_iota(jnp.int32, (rows, SLOTS), 0)
    within = lax.broadcasted_iota(jnp.int32, (rows, SLOTS), 1)
    count = tall * wide
    hot = jnp.where((local == offset + within) & (within < count), 1.0, 0.0).astype(BF16)
    local = lax.broadcasted_iota(jnp.int32, (rows, width), 0)
    is_image = (local >= offset) & (local < offset + count)
    mine_slots = pl.ds(pl.multiple_of(core * SLOTS, SLOTS), SLOTS)
    for c, (ref, text_ref) in enumerate(((ck_ref, tk_ref), (cv_ref, tv_ref))):
        placed = dot(hot, img[c, chip, mine_slots, :], 1, 0)
        ref[...] = jnp.where(is_image, placed, text_ref[...].astype(F32)).astype(BF16)
    for g in range(kv):
        lanes = slice(g * HEAD_DIM, (g + 1) * HEAD_DIM)
        keys = img[0, :, :, lanes].reshape(slots, HEAD_DIM)
        values = img[1, :, :, lanes].reshape(slots, HEAD_DIM)
        for r in range(span // part):
            now, summed, totals = attend(g, r, keys, values, pos_i[...], False)
            done = (summed / totals).astype(BF16)
            for h in range(part // rows):
                at = (g * group + r * (part // rows) + h) * HEAD_DIM
                out_ref[:, at:at + HEAD_DIM] = done[h * rows:(h + 1) * rows]

    loop(1, n, lambda d: info_copy(d).wait_send())
    p1.wait_send()
    loop(1, chips, lambda d: p2_copy(d).wait_send())

    @pl.when(a + 1 < outer)
    def _():
        loop(0, a + 1, lambda f: up_copy(f).wait_send())

    loop(0, a + 1, lambda f: loop(1, inner, lambda d: side_copy(f, d).wait_send()))
    loop(0, a + 1, lambda f: loop(1, inner, lambda d: i_side(f, d).wait_send()))
    loop(0, seen, lambda j: t_mate(j).wait_send())
    loop(a + 1, outer, lambda to: i_copy(to).wait_send())
    loop(0, seen, lambda j: i_mate(j).wait_send())


def body(n, queries, text_keys, text_values, image_features, kv_weight, image_grids):
    chips = n // 2
    inner = 1
    while (2 * inner) ** 2 <= chips and chips % (2 * inner) == 0:
        inner *= 2
    outer = chips // inner
    rows, width = text_keys.shape
    kv = width // HEAD_DIM
    span = queries.shape[1] // width * rows
    slots = image_features.shape[1]
    pair = 2 * SLOTS
    j = np.arange(HEAD_DIM, dtype=np.float64) % (HEAD_DIM // 2)
    freq = jnp.asarray((1000000.0 ** (-2.0 * j / HEAD_DIM)).astype(np.float32)[None, :])
    dma = pltpu.SemaphoreType.DMA
    vmem = pl.BlockSpec(memory_space=pltpu.VMEM)
    smem = pl.BlockSpec(memory_space=pltpu.SMEM)
    hbm = pl.BlockSpec(memory_space=pl.ANY)
    lines = -(-(3 + slots // 128) // 8) * 8
    return pl.pallas_call(
        functools.partial(kernel, n, inner),
        out_shape=(
            jax.ShapeDtypeStruct(queries.shape, BF16),
            jax.ShapeDtypeStruct(text_keys.shape, BF16),
            jax.ShapeDtypeStruct(text_values.shape, BF16),
        ),
        in_specs=[hbm, vmem, vmem, hbm, hbm, smem, vmem],
        out_specs=(vmem,) * 3,
        scratch_shapes=[
            pltpu.VMEM(queries.shape, BF16),
            pltpu.VMEM(image_features.shape, BF16),
            pltpu.VMEM(kv_weight.shape, BF16),
            dma((3,)),
            pltpu.VMEM((n * rows, 2 * width), BF16),
            pltpu.VMEM((2, chips, pair, width), BF16),
            pltpu.VMEM((n, lines, 128), F32),
            pltpu.VMEM((lines, 128), F32),
            pltpu.VMEM((slots, width), F32),
            pltpu.VMEM((slots, width), BF16),
            pltpu.VMEM((slots, width), BF16),
            pltpu.VMEM((slots, width), BF16),
            pltpu.VMEM((chips, pair, width), BF16),
            pltpu.VMEM((kv, span, HEAD_DIM), BF16),
            pltpu.VMEM((1, n * rows), jnp.int32),
            pltpu.VMEM((1, slots), jnp.int32),
            pltpu.VMEM((kv, span, HEAD_DIM), F32),
            pltpu.VMEM((kv, span, 2 * HEAD_DIM), F32),
            dma((n,)), dma((n,)), dma, dma, dma((chips,)), dma((chips,)),
            dma((outer,)), dma((chips,)), dma((chips,)), dma((chips,)), dma((chips,)),
            dma((outer,)), dma((chips,)), dma((chips,)), dma((chips,)), dma((chips,)),
        ],
        compiler_params=pltpu.CompilerParams(
            collective_id=0, has_side_effects=True, vmem_limit_bytes=60 * 1024 * 1024
        ),
        cost_estimate=pl.CostEstimate(
            flops=4 * n * rows * queries.size, bytes_accessed=4 * queries.size,
            transcendentals=n * rows * rows * 32),
    )(queries, text_keys, text_values, image_features, kv_weight, image_grids, freq)


def solution(mesh):
    both = P(("groups", "ctx"), None)
    return jax.shard_map(
        functools.partial(body, mesh.shape["ctx"]), mesh=mesh,
        in_specs=(both, both, both, both, P("ctx", None), both),
        out_specs=(both, both, both), check_vma=False)
```

```python
import functools
import math

import jax
import jax.numpy as jnp
import numpy as np
from jax import lax
from jax.experimental import pallas as pl
from jax.experimental.pallas import tpu as pltpu
from jax.sharding import PartitionSpec as P

HEAD_DIM = 128
GRID = 4
SLOTS = GRID * GRID
BIG = 1 << 30
NEG = -1e30
F32 = jnp.float32
BF16 = jnp.bfloat16


def dot(x, y, cx, cy):
    return lax.dot_general(x, y, (((cx,), (cy,)), ((), ())), preferred_element_type=F32)


def kernel(
    n, inner,
    q_hbm, tk_ref, tv_ref, feat_hbm, w_hbm, grid_ref, freq_ref,
    out_ref, ck_ref, cv_ref,
    q_ref, feat_ref, w_ref, load_s, tkv, img, info, info_sum, mine, p1_src, p1_dst, p2_src, p2_dst, qs, pos_t, pos_i, m_ref, acc_ref,
    info_s, info_r, p1_s, p1_r, p2_s, p2_r,
    tz_s, ty_s, t_r, tm_s, tm_r, i_s, is_s, i_r, im_s, im_r,
):
    chips = n // 2
    outer = chips // inner
    rows, width = tk_ref.shape
    kv = width // HEAD_DIM
    group = q_ref.shape[1] // width
    feats, slots = feat_ref.shape
    pair = 2 * SLOTS
    total_features = feats * n
    me = lax.axis_index("ctx")
    core = lax.rem(me, 2)
    chip = me // 2
    a = chip // inner
    b = lax.rem(chip, inner)
    mate = me + 1 - 2 * core

    def loop(low, high, f):
        lax.fori_loop(low, high, lambda i, c: (f(i), c)[1], 0)

    def copy(src, dst, send, recv, target):
        return pltpu.make_async_remote_copy(
            src_ref=src, dst_ref=dst, send_sem=send, recv_sem=recv,
            device_id={"ctx": target}, device_id_type=pl.DeviceIdType.MESH,
        )

    loads = [pltpu.make_async_copy(src, dst, load_s.at[i]) for i, (src, dst) in enumerate(
        ((feat_hbm, feat_ref), (w_hbm, w_ref), (q_hbm, q_ref)))]
    for load in loads:
        load.start()

    own = pl.ds(pl.multiple_of(me * rows, rows), rows)
    tkv[:, width:] = jnp.zeros((n * rows, width), BF16)
    tkv[own, :width] = tk_ref[...]
    tkv[own, width:] = tv_ref[...]
    offset, tall, wide = grid_ref[0, 0], grid_ref[0, 1], grid_ref[0, 2]
    img[...] = jnp.zeros_like(img)

    barrier = pltpu.get_barrier_semaphore()
    loop(1, n, lambda d: pl.semaphore_signal(
        barrier, inc=1, device_id={"ctx": lax.rem(me + d, n)},
        device_id_type=pl.DeviceIdType.MESH))
    pl.semaphore_wait(barrier, n - 1)

    def block(j):
        shard = 2 * j + core
        return tkv.at[pl.ds(pl.multiple_of(shard * rows, rows), rows), :]

    def info_copy(d):
        return copy(info.at[me], info.at[me], info_s.at[d], info_r.at[me], lax.rem(me + d, n))

    def info_in(j):
        return copy(info.at[j], info.at[j], info_s.at[0], info_r.at[j], mate)

    def up_copy(from_a):
        j = from_a * inner + b
        return copy(block(j), block(j), tz_s.at[from_a], t_r.at[j], me + 2 * inner)

    def side_copy(from_a, d):
        j = from_a * inner + b
        return copy(block(j), block(j), ty_s.at[from_a * inner + d], t_r.at[j],
                    2 * (a * inner + lax.rem(b + d, inner)) + core)

    def t_in(j):
        return copy(block(j), block(j), tz_s.at[0], t_r.at[j], mate)

    def t_mate(j):
        return copy(block(j), block(j), tm_s.at[j], tm_r.at[j], mate)

    def t_mate_in(j):
        shard = 2 * j + 1 - core
        ref = tkv.at[pl.ds(pl.multiple_of(shard * rows, rows), rows), :]
        return copy(ref, ref, tm_s.at[j], tm_r.at[j], mate)

    @pl.when(a + 1 < outer)
    def _():
        up_copy(a).start()

    loop(1, inner, lambda d: side_copy(a, d).start())
    t_mate(chip).start()

    half = lambda c: w_ref[:, pl.ds(pl.multiple_of(c * width, width), width)]
    loads[0].wait()
    features = feat_ref[...].T
    loads[1].wait()
    p1_src[...] = dot(features, half(1 - core), 1, 0).astype(BF16)
    p1 = copy(p1_src, p1_dst, p1_s, p1_r, mate)
    p1.start()
    mine[...] = dot(features, half(core), 1, 0)

    wide_f = feat_ref[...].astype(F32)
    power = jnp.sum(wide_f * wide_f, axis=0, keepdims=True)
    line = lax.broadcasted_iota(jnp.int32, info.shape[1:], 0)
    facts = jnp.where(line == 0, offset, jnp.where(line == 1, tall, wide)).astype(F32)
    for i in range(slots // 128):
        facts = jnp.where(line == 3 + i, power[:, i * 128:(i + 1) * 128], facts)
    info[me] = facts
    loop(1, n, lambda d: info_copy(d).start())

    p1.wait_recv()
    both_cores = mine[...] + p1_dst[...].astype(F32)
    mine[...] = both_cores
    p2_src[...] = both_cores.astype(BF16)

    def pass_on(i):
        from_a = a - 1 - i
        j = from_a * inner + b
        t_in(j).wait_recv()

        @pl.when(a + 1 < outer)
        def _():
            up_copy(from_a).start()

        loop(1, inner, lambda d: side_copy(from_a, d).start())
        t_mate(j).start()

    first_on = jnp.minimum(a, 1)

    def p2_copy(d):
        j = lax.rem(chip + d, chips)
        return copy(p2_src.at[pl.ds(pl.multiple_of(j * pair, pair), pair), :], p2_dst.at[chip],
                    p2_s.at[d], p2_r.at[chip], 2 * j + core)

    def p2_in(j):
        return copy(p2_dst.at[j], p2_dst.at[j], p2_s.at[0], p2_r.at[j], mate)

    loop(0, first_on, pass_on)
    loop(1, chips, lambda d: p2_copy(d).start())

    loads[2].wait()
    for g in range(kv):
        for h in range(group):
            at = (g * group + h) * HEAD_DIM
            qs[g, h * rows:(h + 1) * rows, :] = q_ref[:, at:at + HEAD_DIM]

    def gather_facts(d, total):
        j = lax.rem(me + d, n)
        info_in(j).wait_recv()
        return total + info[j]

    info_sum[...] = lax.fori_loop(1, n, gather_facts, info[me])

    row = lax.broadcasted_iota(jnp.int32, (pair, 128), 0)
    lane = lax.broadcasted_iota(jnp.int32, (pair, 128), 1)
    second = row >= SLOTS
    k = jnp.where(second, row - SLOTS, row)
    pick = lambda i: jnp.where(
        second, info[2 * chip + 1, i:i + 1, :], info[2 * chip, i:i + 1, :]).astype(jnp.int32)
    gw = pick(2)
    gy = jnp.zeros_like(k)
    for i in range(1, SLOTS // 2):
        gy = gy + jnp.where(k >= i * gw, 1, 0)
    gx = k - gy * gw
    t_id = (2 * chip + jnp.where(second, 1, 0)) * rows + pick(0)
    j = jnp.where(lane >= HEAD_DIM // 2, lane - HEAD_DIM // 2, lane)
    first_bound = HEAD_DIM // 8
    second_bound = first_bound + 3 * HEAD_DIM // 16
    ids = t_id + jnp.where(j < first_bound, 0, jnp.where(j < second_bound, gy, gx))
    angle = ids.astype(F32) * freq_ref[...]
    is_key = core == 0
    cosine = jnp.where(is_key, jnp.cos(angle), 1.0)
    sine = jnp.where(is_key, jnp.sin(angle), 0.0)
    sine = jnp.where(lane < HEAD_DIM // 2, -sine, sine)

    loop(first_on, a, pass_on)

    mine_rows = pl.ds(pl.multiple_of(chip * pair, pair), pair)

    def add(d, total):
        src = lax.rem(chip + d, chips)
        p2_in(src).wait_recv()
        return total + p2_dst[src].astype(F32)

    total = lax.fori_loop(1, chips, add, mine[mine_rows, :])
    squares = info_sum[pl.ds(3 + chip * pair // 128, 1), :]
    squares = jnp.where(lane == lax.rem(chip * pair, 128) + row, squares, 0.0)
    power = jnp.sum(squares, axis=1, keepdims=True)
    scale = lax.rsqrt(power / total_features + 1e-6)
    for h in range(kv):
        at = slice(h * HEAD_DIM, (h + 1) * HEAD_DIM)
        x = total[:, at] * scale
        turned = jnp.concatenate([x[:, HEAD_DIM // 2:], x[:, :HEAD_DIM // 2]], axis=1)
        img[core, chip, :, at] = (x * cosine + turned * sine).astype(BF16)

    def i_copy(to_a):
        return copy(img.at[core, chip], img.at[core, chip], i_s.at[to_a], i_r.at[chip],
                    2 * (to_a * inner + b) + core)

    def i_side(from_a, d):
        j = from_a * inner + b
        return copy(img.at[core, j], img.at[core, j], is_s.at[from_a * inner + d], i_r.at[j],
                    2 * (a * inner + lax.rem(b + d, inner)) + core)

    def i_in(j):
        return copy(img.at[core, j], img.at[core, j], i_s.at[0], i_r.at[j], mate)

    def i_mate(j):
        return copy(img.at[core, j], img.at[core, j], im_s.at[j], im_r.at[j], mate)

    def i_mate_in(j):
        return copy(img.at[1 - core, j], img.at[1 - core, j], im_s.at[j], im_r.at[j], mate)

    seen = (a + 1) * inner
    loop(a + 1, outer, lambda to: i_copy(to).start())
    loop(1, inner, lambda d: i_side(a, d).start())
    i_mate(chip).start()
    def from_side(from_a):
        def step(d):
            j = from_a * inner + lax.rem(b + d, inner)
            t_in(j).wait_recv()
            t_mate(j).start()

        loop(1, inner, step)

    lane_t = lax.broadcasted_iota(jnp.int32, pos_t.shape, 1)
    lane_i = lax.broadcasted_iota(jnp.int32, pos_i.shape, 1)

    def place(j, carry):
        text, image = carry
        o, t, w = (info[j, i:i + 1, 0:1].astype(jnp.int32) for i in range(3))
        begin = j * rows + o
        dead = (lane_t >= begin) & (lane_t < begin + t * w)
        k = lane_i - j * SLOTS
        live = (k >= 0) & (k < t * w)
        return jnp.where(dead, BIG, text), jnp.where(live, begin + k, image)

    text, image = lax.fori_loop(0, n, place, (lane_t, jnp.full(pos_i.shape, BIG, jnp.int32)))
    pos_t[...] = text
    pos_i[...] = image

    span = group * rows
    part = math.gcd(span, 256)
    plane = 2 * inner * rows
    block_keys = max(plane, math.gcd(n * rows, 512))
    planes = block_keys // plane
    last = a // planes
    factor = math.log2(math.e) / math.sqrt(HEAD_DIM)
    q_pos = me * rows + lax.rem(lax.broadcasted_iota(jnp.int32, (part, 1), 0), rows)

    def attend(g, r, keys, values, pos, first):
        at = slice(r * part, (r + 1) * part)
        s = dot(qs[g, at, :], keys, 1, 1)
        s = jnp.where(pos <= q_pos, s, NEG)
        now = jnp.broadcast_to(jnp.max(s, axis=1, keepdims=True), (part, HEAD_DIM))
        if not first:
            before = m_ref[g, at, :]
            now = jnp.maximum(before, now)
        shift = jnp.concatenate([now] * (s.shape[1] // HEAD_DIM), axis=1)
        weight = jnp.exp2((s - shift) * factor).astype(BF16)
        both = jnp.concatenate([values, jnp.ones_like(values)], axis=1)
        product = dot(weight, both, 1, 0)
        summed, totals = product[:, :HEAD_DIM], product[:, HEAD_DIM:]
        if not first:
            shrink = jnp.exp2((before - now) * factor)
            summed = summed + acc_ref[g, at, :HEAD_DIM] * shrink
            totals = totals + acc_ref[g, at, HEAD_DIM:] * shrink
        return now, summed, totals

    def text_block(g, r, p, first):
        at = pl.ds(pl.multiple_of(p * block_keys, block_keys), block_keys)
        lo = g * HEAD_DIM
        now, summed, totals = attend(
            g, r, tkv[at, lo:lo + HEAD_DIM], tkv[at, width + lo:width + lo + HEAD_DIM],
            pos_t[:, at], first)
        at = slice(r * part, (r + 1) * part)
        m_ref[g, at, :] = now
        acc_ref[g, at, :HEAD_DIM] = summed
        acc_ref[g, at, HEAD_DIM:] = totals

    def text_heads(heads, p, first):
        for g in heads:
            for r in range(span // part):
                text_block(g, r, p, first)

    def text_wait(p):
        low = p * planes * inner
        high = jnp.minimum(seen, low + planes * inner)
        loop(low, high, lambda j: t_mate_in(j).wait_recv())

    def image_on(from_a):
        j = from_a * inner + b
        i_in(j).wait_recv()
        loop(1, inner, lambda d: i_side(from_a, d).start())
        i_mate(j).start()

    def image_from_side(from_a):
        def step(d):
            j = from_a * inner + lax.rem(b + d, inner)
            i_in(j).wait_recv()
            i_mate(j).start()

        loop(1, inner, step)

    def images_on():
        loop(0, a, image_on)

    def images_from_side():
        loop(0, a + 1, image_from_side)

    low = last * planes
    loop(0, a + 1 - low, lambda i: from_side(a - i))
    text_wait(last)
    text_heads(range(kv // 2), last, True)
    loop(0, low, lambda i: from_side(low - 1 - i))
    text_heads(range(kv // 2, kv - 1), last, True)
    images_on()
    text_heads(range(kv - 1, kv), last, True)

    def more(i):
        p = last - 1 - i
        text_wait(p)
        text_heads(range(kv // 2), p, False)

        @pl.when(p == 0)
        def _():
            images_from_side()

        text_heads(range(kv // 2, kv), p, False)

    loop(0, last, more)

    @pl.when(last == 0)
    def _():
        images_from_side()

    loop(0, seen, lambda j: i_mate_in(j).wait_recv())
    local = lax.broadcasted_iota(jnp.int32, (rows, SLOTS), 0)
    within = lax.broadcasted_iota(jnp.int32, (rows, SLOTS), 1)
    count = tall * wide
    hot = jnp.where((local == offset + within) & (within < count), 1.0, 0.0).astype(BF16)
    local = lax.broadcasted_iota(jnp.int32, (rows, width), 0)
    is_image = (local >= offset) & (local < offset + count)
    mine_slots = pl.ds(pl.multiple_of(core * SLOTS, SLOTS), SLOTS)
    for c, (ref, text_ref) in enumerate(((ck_ref, tk_ref), (cv_ref, tv_ref))):
        placed = dot(hot, img[c, chip, mine_slots, :], 1, 0)
        ref[...] = jnp.where(is_image, placed, text_ref[...].astype(F32)).astype(BF16)
    for g in range(kv):
        lanes = slice(g * HEAD_DIM, (g + 1) * HEAD_DIM)
        keys = img[0, :, :, lanes].reshape(slots, HEAD_DIM)
        values = img[1, :, :, lanes].reshape(slots, HEAD_DIM)
        for r in range(span // part):
            now, summed, totals = attend(g, r, keys, values, pos_i[...], False)
            done = (summed / totals).astype(BF16)
            for h in range(part // rows):
                at = (g * group + r * (part // rows) + h) * HEAD_DIM
                out_ref[:, at:at + HEAD_DIM] = done[h * rows:(h + 1) * rows]

    loop(1, n, lambda d: info_copy(d).wait_send())
    p1.wait_send()
    loop(1, chips, lambda d: p2_copy(d).wait_send())

    @pl.when(a + 1 < outer)
    def _():
        loop(0, a + 1, lambda f: up_copy(f).wait_send())

    loop(0, a + 1, lambda f: loop(1, inner, lambda d: side_copy(f, d).wait_send()))
    loop(0, a + 1, lambda f: loop(1, inner, lambda d: i_side(f, d).wait_send()))
    loop(0, seen, lambda j: t_mate(j).wait_send())
    loop(a + 1, outer, lambda to: i_copy(to).wait_send())
    loop(0, seen, lambda j: i_mate(j).wait_send())


def body(n, queries, text_keys, text_values, image_features, kv_weight, image_grids):
    chips = n // 2
    inner = 1
    while (2 * inner) ** 2 <= chips and chips % (2 * inner) == 0:
        inner *= 2
    outer = chips // inner
    rows, width = text_keys.shape
    kv = width // HEAD_DIM
    span = queries.shape[1] // width * rows
    slots = image_features.shape[1]
    pair = 2 * SLOTS
    j = np.arange(HEAD_DIM, dtype=np.float64) % (HEAD_DIM // 2)
    freq = jnp.asarray((1000000.0 ** (-2.0 * j / HEAD_DIM)).astype(np.float32)[None, :])
    dma = pltpu.SemaphoreType.DMA
    vmem = pl.BlockSpec(memory_space=pltpu.VMEM)
    smem = pl.BlockSpec(memory_space=pltpu.SMEM)
    hbm = pl.BlockSpec(memory_space=pl.ANY)
    lines = -(-(3 + slots // 128) // 8) * 8
    return pl.pallas_call(
        functools.partial(kernel, n, inner),
        out_shape=(
            jax.ShapeDtypeStruct(queries.shape, BF16),
            jax.ShapeDtypeStruct(text_keys.shape, BF16),
            jax.ShapeDtypeStruct(text_values.shape, BF16),
        ),
        in_specs=[hbm, vmem, vmem, hbm, hbm, smem, vmem],
        out_specs=(vmem,) * 3,
        scratch_shapes=[
            pltpu.VMEM(queries.shape, BF16),
            pltpu.VMEM(image_features.shape, BF16),
            pltpu.VMEM(kv_weight.shape, BF16),
            dma((3,)),
            pltpu.VMEM((n * rows, 2 * width), BF16),
            pltpu.VMEM((2, chips, pair, width), BF16),
            pltpu.VMEM((n, lines, 128), F32),
            pltpu.VMEM((lines, 128), F32),
            pltpu.VMEM((slots, width), F32),
            pltpu.VMEM((slots, width), BF16),
            pltpu.VMEM((slots, width), BF16),
            pltpu.VMEM((slots, width), BF16),
            pltpu.VMEM((chips, pair, width), BF16),
            pltpu.VMEM((kv, span, HEAD_DIM), BF16),
            pltpu.VMEM((1, n * rows), jnp.int32),
            pltpu.VMEM((1, slots), jnp.int32),
            pltpu.VMEM((kv, span, HEAD_DIM), F32),
            pltpu.VMEM((kv, span, 2 * HEAD_DIM), F32),
            dma((n,)), dma((n,)), dma, dma, dma((chips,)), dma((chips,)),
            dma((outer,)), dma((chips,)), dma((chips,)), dma((chips,)), dma((chips,)),
            dma((outer,)), dma((chips,)), dma((chips,)), dma((chips,)), dma((chips,)),
        ],
        compiler_params=pltpu.CompilerParams(
            collective_id=0, has_side_effects=True, vmem_limit_bytes=60 * 1024 * 1024
        ),
        cost_estimate=pl.CostEstimate(
            flops=4 * n * rows * queries.size, bytes_accessed=4 * queries.size,
            transcendentals=n * rows * rows * 32),
    )(queries, text_keys, text_values, image_features, kv_weight, image_grids, freq)


def solution(mesh):
    both = P(("groups", "ctx"), None)
    return jax.shard_map(
        functools.partial(body, mesh.shape["ctx"]), mesh=mesh,
        in_specs=(both, both, both, both, P("ctx", None), both),
        out_specs=(both, both, both), check_vma=False)
```

```python
import functools
import math

import jax
import jax.numpy as jnp
import numpy as np
from jax import lax
from jax.experimental import pallas as pl
from jax.experimental.pallas import tpu as pltpu
from jax.sharding import PartitionSpec as P

HEAD_DIM = 128
GRID = 4
SLOTS = GRID * GRID
BIG = 1 << 30
NEG = -1e30
F32 = jnp.float32
BF16 = jnp.bfloat16


def dot(x, y, cx, cy):
    return lax.dot_general(x, y, (((cx,), (cy,)), ((), ())), preferred_element_type=F32)


def kernel(
    n, inner,
    q_hbm, tk_ref, tv_ref, feat_hbm, w_hbm, grid_ref, freq_ref,
    out_ref, ck_ref, cv_ref,
    q_ref, feat_ref, w_ref, load_s, tkv, img, info, info_sum, mine, p1_src, p1_dst, p2_src, p2_dst, p3_src, p3_dst, qs, pos_t, pos_i, m_ref, acc_ref,
    info_s, info_r, p1_s, p1_r, p2_s, p2_r, p3_s, p3_r,
    tz_s, ty_s, t_r, tm_s, tm_r, i_s, is_s, i_r, im_s, im_r,
):
    chips = n // 2
    outer = chips // inner
    rows, width = tk_ref.shape
    kv = width // HEAD_DIM
    group = q_ref.shape[1] // width
    feats, slots = feat_ref.shape
    pair = 2 * SLOTS
    total_features = feats * n
    me = lax.axis_index("ctx")
    core = lax.rem(me, 2)
    chip = me // 2
    a = chip // inner
    b = lax.rem(chip, inner)
    mate = me + 1 - 2 * core

    def loop(low, high, f):
        lax.fori_loop(low, high, lambda i, c: (f(i), c)[1], 0)

    def copy(src, dst, send, recv, target):
        return pltpu.make_async_remote_copy(
            src_ref=src, dst_ref=dst, send_sem=send, recv_sem=recv,
            device_id={"ctx": target}, device_id_type=pl.DeviceIdType.MESH,
        )

    loads = [pltpu.make_async_copy(src, dst, load_s.at[i]) for i, (src, dst) in enumerate(
        ((feat_hbm, feat_ref), (w_hbm, w_ref), (q_hbm, q_ref)))]
    for load in loads:
        load.start()

    own = pl.ds(pl.multiple_of(me * rows, rows), rows)
    tkv[:, width:] = jnp.zeros((n * rows, width), BF16)
    tkv[own, :width] = tk_ref[...]
    tkv[own, width:] = tv_ref[...]
    offset, tall, wide = grid_ref[0, 0], grid_ref[0, 1], grid_ref[0, 2]
    img[...] = jnp.zeros_like(img)

    barrier = pltpu.get_barrier_semaphore()
    loop(1, n, lambda d: pl.semaphore_signal(
        barrier, inc=1, device_id={"ctx": lax.rem(me + d, n)},
        device_id_type=pl.DeviceIdType.MESH))
    pl.semaphore_wait(barrier, n - 1)

    def block(j):
        shard = 2 * j + core
        return tkv.at[pl.ds(pl.multiple_of(shard * rows, rows), rows), :]

    def info_copy(d):
        return copy(info.at[me], info.at[me], info_s.at[d], info_r.at[me], lax.rem(me + d, n))

    def info_in(j):
        return copy(info.at[j], info.at[j], info_s.at[0], info_r.at[j], mate)

    def up_copy(from_a):
        j = from_a * inner + b
        return copy(block(j), block(j), tz_s.at[from_a], t_r.at[j], me + 2 * inner)

    def side_copy(from_a, d):
        j = from_a * inner + b
        return copy(block(j), block(j), ty_s.at[from_a * inner + d], t_r.at[j],
                    2 * (a * inner + lax.rem(b + d, inner)) + core)

    def t_in(j):
        return copy(block(j), block(j), tz_s.at[0], t_r.at[j], mate)

    def t_mate(j):
        return copy(block(j), block(j), tm_s.at[j], tm_r.at[j], mate)

    def t_mate_in(j):
        shard = 2 * j + 1 - core
        ref = tkv.at[pl.ds(pl.multiple_of(shard * rows, rows), rows), :]
        return copy(ref, ref, tm_s.at[j], tm_r.at[j], mate)

    @pl.when(a + 1 < outer)
    def _():
        up_copy(a).start()

    loop(1, inner, lambda d: side_copy(a, d).start())
    t_mate(chip).start()

    half = lambda c: w_ref[:, pl.ds(pl.multiple_of(c * width, width), width)]
    loads[0].wait()
    features = feat_ref[...].T
    loads[1].wait()
    p1_src[...] = dot(features, half(1 - core), 1, 0).astype(BF16)
    p1 = copy(p1_src, p1_dst, p1_s, p1_r, mate)
    p1.start()
    mine[...] = dot(features, half(core), 1, 0)

    wide_f = feat_ref[...].astype(F32)
    power = jnp.sum(wide_f * wide_f, axis=0, keepdims=True)
    line = lax.broadcasted_iota(jnp.int32, info.shape[1:], 0)
    facts = jnp.where(line == 0, offset, jnp.where(line == 1, tall, wide)).astype(F32)
    for i in range(slots // 128):
        facts = jnp.where(line == 3 + i, power[:, i * 128:(i + 1) * 128], facts)
    info[me] = facts
    loop(1, n, lambda d: info_copy(d).start())

    p1.wait_recv()
    both_cores = mine[...] + p1_dst[...].astype(F32)
    mine[...] = both_cores
    for j in range(chips):
        to = (j % inner * outer + j // inner) * pair
        p2_src[to:to + pair, :] = both_cores[j * pair:(j + 1) * pair].astype(BF16)

    def pass_on(i):
        from_a = a - 1 - i
        j = from_a * inner + b
        t_in(j).wait_recv()

        @pl.when(a + 1 < outer)
        def _():
            up_copy(from_a).start()

        loop(1, inner, lambda d: side_copy(from_a, d).start())
        t_mate(j).start()

    first_on = jnp.minimum(a, 1)

    column = outer * pair

    def p2_copy(d):
        to_b = lax.rem(b + d, inner)
        return copy(p2_src.at[pl.ds(pl.multiple_of(to_b * column, column), column), :],
                    p2_dst.at[b], p2_s.at[d], p2_r.at[b], 2 * (a * inner + to_b) + core)

    def p2_in(j):
        return copy(p2_dst.at[j], p2_dst.at[j], p2_s.at[0], p2_r.at[j], mate)

    def p3_copy(d):
        to_a = lax.rem(a + d, outer)
        return copy(p3_src.at[to_a], p3_dst.at[a], p3_s.at[d], p3_r.at[a],
                    2 * (to_a * inner + b) + core)

    def p3_in(j):
        return copy(p3_dst.at[j], p3_dst.at[j], p3_s.at[0], p3_r.at[j], mate)

    def column_sum(of_a):
        at = pl.ds(pl.multiple_of((of_a * inner + b) * pair, pair), pair)
        total = mine[at, :]
        at = pl.ds(pl.multiple_of(of_a * pair, pair), pair)
        return lax.fori_loop(
            1, inner,
            lambda d, x: x + p2_dst[lax.rem(b + d, inner), at, :].astype(F32), total)

    loop(1, inner, lambda d: p2_copy(d).start())
    loop(0, first_on, pass_on)
    loop(1, inner, lambda d: p2_in(lax.rem(b + d, inner)).wait_recv())

    def send_sum(d):
        to_a = lax.rem(a + d, outer)
        p3_src[to_a] = column_sum(to_a).astype(BF16)
        p3_copy(d).start()

    loop(1, outer, send_sum)

    loads[2].wait()
    for g in range(kv):
        for h in range(group):
            at = (g * group + h) * HEAD_DIM
            qs[g, h * rows:(h + 1) * rows, :] = q_ref[:, at:at + HEAD_DIM]

    def gather_facts(d, total):
        j = lax.rem(me + d, n)
        info_in(j).wait_recv()
        return total + info[j]

    info_sum[...] = lax.fori_loop(1, n, gather_facts, info[me])

    row = lax.broadcasted_iota(jnp.int32, (pair, 128), 0)
    lane = lax.broadcasted_iota(jnp.int32, (pair, 128), 1)
    second = row >= SLOTS
    k = jnp.where(second, row - SLOTS, row)
    pick = lambda i: jnp.where(
        second, info[2 * chip + 1, i:i + 1, :], info[2 * chip, i:i + 1, :]).astype(jnp.int32)
    gw = pick(2)
    gy = jnp.zeros_like(k)
    for i in range(1, SLOTS // 2):
        gy = gy + jnp.where(k >= i * gw, 1, 0)
    gx = k - gy * gw
    t_id = (2 * chip + jnp.where(second, 1, 0)) * rows + pick(0)
    j = jnp.where(lane >= HEAD_DIM // 2, lane - HEAD_DIM // 2, lane)
    first_bound = HEAD_DIM // 8
    second_bound = first_bound + 3 * HEAD_DIM // 16
    ids = t_id + jnp.where(j < first_bound, 0, jnp.where(j < second_bound, gy, gx))
    angle = ids.astype(F32) * freq_ref[...]
    is_key = core == 0
    cosine = jnp.where(is_key, jnp.cos(angle), 1.0)
    sine = jnp.where(is_key, jnp.sin(angle), 0.0)
    sine = jnp.where(lane < HEAD_DIM // 2, -sine, sine)

    loop(first_on, a, pass_on)

    lane_t = lax.broadcasted_iota(jnp.int32, pos_t.shape, 1)
    lane_i = lax.broadcasted_iota(jnp.int32, pos_i.shape, 1)
    shard_t = lane_t // rows
    shard_i = lane_i // SLOTS

    def place(j, carry):
        text, image = carry
        code = info[j, 0:1, :] * 64.0 + info[j, 1:2, :] * info[j, 2:3, :]
        spread = lambda x: jnp.concatenate([code] * (x.shape[1] // 128), axis=1)
        return (jnp.where(shard_t == j, spread(text), text),
                jnp.where(shard_i == j, spread(image), image))

    text, image = lax.fori_loop(
        0, n, place, (jnp.zeros(pos_t.shape, F32), jnp.zeros(pos_i.shape, F32)))
    text, image = text.astype(jnp.int32), image.astype(jnp.int32)
    within = lane_t - shard_t * rows - text // 64
    pos_t[...] = jnp.where((within >= 0) & (within < text % 64), BIG, lane_t)
    within = lane_i - shard_i * SLOTS
    pos_i[...] = jnp.where(
        within < image % 64, shard_i * rows + image // 64 + within, BIG)

    def add(d, total):
        src = lax.rem(a + d, outer)
        p3_in(src).wait_recv()
        return total + p3_dst[src].astype(F32)

    total = lax.fori_loop(1, outer, add, column_sum(a))
    squares = info_sum[pl.ds(3 + chip * pair // 128, 1), :]
    squares = jnp.where(lane == lax.rem(chip * pair, 128) + row, squares, 0.0)
    power = jnp.sum(squares, axis=1, keepdims=True)
    scale = lax.rsqrt(power / total_features + 1e-6)
    for h in range(kv):
        at = slice(h * HEAD_DIM, (h + 1) * HEAD_DIM)
        x = total[:, at] * scale
        turned = jnp.concatenate([x[:, HEAD_DIM // 2:], x[:, :HEAD_DIM // 2]], axis=1)
        img[core, chip, :, at] = (x * cosine + turned * sine).astype(BF16)

    def i_copy(to_a):
        return copy(img.at[core, chip], img.at[core, chip], i_s.at[to_a], i_r.at[chip],
                    2 * (to_a * inner + b) + core)

    def i_side(from_a, d):
        j = from_a * inner + b
        return copy(img.at[core, j], img.at[core, j], is_s.at[from_a * inner + d], i_r.at[j],
                    2 * (a * inner + lax.rem(b + d, inner)) + core)

    def i_in(j):
        return copy(img.at[core, j], img.at[core, j], i_s.at[0], i_r.at[j], mate)

    def i_mate(j):
        return copy(img.at[core, j], img.at[core, j], im_s.at[j], im_r.at[j], mate)

    def i_mate_in(j):
        return copy(img.at[1 - core, j], img.at[1 - core, j], im_s.at[j], im_r.at[j], mate)

    seen = (a + 1) * inner
    loop(a + 1, outer, lambda to: i_copy(to).start())
    loop(1, inner, lambda d: i_side(a, d).start())
    i_mate(chip).start()
    def from_side(from_a):
        def step(d):
            j = from_a * inner + lax.rem(b + d, inner)
            t_in(j).wait_recv()
            t_mate(j).start()

        loop(1, inner, step)

    span = group * rows
    part = math.gcd(span, 256)
    plane = 2 * inner * rows
    block_keys = max(plane, math.gcd(n * rows, 512))
    planes = block_keys // plane
    last = a // planes
    factor = math.log2(math.e) / math.sqrt(HEAD_DIM)
    q_pos = me * rows + lax.rem(lax.broadcasted_iota(jnp.int32, (part, 1), 0), rows)

    def attend(g, r, keys, values, pos, first):
        at = slice(r * part, (r + 1) * part)
        s = dot(qs[g, at, :], keys, 1, 1)
        s = jnp.where(pos <= q_pos, s, NEG)
        now = jnp.broadcast_to(jnp.max(s, axis=1, keepdims=True), (part, HEAD_DIM))
        if not first:
            before = m_ref[g, at, :]
            now = jnp.maximum(before, now)
        shift = jnp.concatenate([now] * (s.shape[1] // HEAD_DIM), axis=1)
        weight = jnp.exp2((s - shift) * factor).astype(BF16)
        both = jnp.concatenate([values, jnp.ones_like(values)], axis=1)
        product = dot(weight, both, 1, 0)
        summed, totals = product[:, :HEAD_DIM], product[:, HEAD_DIM:]
        if not first:
            shrink = jnp.exp2((before - now) * factor)
            summed = summed + acc_ref[g, at, :HEAD_DIM] * shrink
            totals = totals + acc_ref[g, at, HEAD_DIM:] * shrink
        return now, summed, totals

    def text_block(g, r, p, first):
        at = pl.ds(pl.multiple_of(p * block_keys, block_keys), block_keys)
        lo = g * HEAD_DIM
        now, summed, totals = attend(
            g, r, tkv[at, lo:lo + HEAD_DIM], tkv[at, width + lo:width + lo + HEAD_DIM],
            pos_t[:, at], first)
        at = slice(r * part, (r + 1) * part)
        m_ref[g, at, :] = now
        acc_ref[g, at, :HEAD_DIM] = summed
        acc_ref[g, at, HEAD_DIM:] = totals

    def text_heads(heads, p, first):
        for g in heads:
            for r in range(span // part):
                text_block(g, r, p, first)

    def text_wait(p):
        low = p * planes * inner
        high = jnp.minimum(seen, low + planes * inner)
        loop(low, high, lambda j: t_mate_in(j).wait_recv())

    def image_on(from_a):
        j = from_a * inner + b
        i_in(j).wait_recv()
        loop(1, inner, lambda d: i_side(from_a, d).start())
        i_mate(j).start()

    def image_from_side(from_a):
        def step(d):
            j = from_a * inner + lax.rem(b + d, inner)
            i_in(j).wait_recv()
            i_mate(j).start()

        loop(1, inner, step)

    def images_on():
        loop(0, a, image_on)

    def images_from_side():
        loop(0, a + 1, image_from_side)

    low = last * planes
    loop(0, a + 1 - low, lambda i: from_side(a - i))
    text_wait(last)
    text_heads(range(kv // 2), last, True)
    loop(0, low, lambda i: from_side(low - 1 - i))
    text_heads(range(kv // 2, kv - 1), last, True)
    images_on()
    text_heads(range(kv - 1, kv), last, True)

    def more(i):
        p = last - 1 - i
        text_wait(p)
        text_heads(range(kv // 2), p, False)

        @pl.when(p == 0)
        def _():
            images_from_side()

        text_heads(range(kv // 2, kv), p, False)

    loop(0, last, more)

    @pl.when(last == 0)
    def _():
        images_from_side()

    loop(0, seen, lambda j: i_mate_in(j).wait_recv())
    local = lax.broadcasted_iota(jnp.int32, (rows, SLOTS), 0)
    within = lax.broadcasted_iota(jnp.int32, (rows, SLOTS), 1)
    count = tall * wide
    hot = jnp.where((local == offset + within) & (within < count), 1.0, 0.0).astype(BF16)
    local = lax.broadcasted_iota(jnp.int32, (rows, width), 0)
    is_image = (local >= offset) & (local < offset + count)
    mine_slots = pl.ds(pl.multiple_of(core * SLOTS, SLOTS), SLOTS)
    for c, (ref, text_ref) in enumerate(((ck_ref, tk_ref), (cv_ref, tv_ref))):
        placed = dot(hot, img[c, chip, mine_slots, :], 1, 0)
        ref[...] = jnp.where(is_image, placed, text_ref[...].astype(F32)).astype(BF16)
    for g in range(kv):
        lanes = slice(g * HEAD_DIM, (g + 1) * HEAD_DIM)
        keys = img[0, :, :, lanes].reshape(slots, HEAD_DIM)
        values = img[1, :, :, lanes].reshape(slots, HEAD_DIM)
        for r in range(span // part):
            now, summed, totals = attend(g, r, keys, values, pos_i[...], False)
            done = (summed / totals).astype(BF16)
            for h in range(part // rows):
                at = (g * group + r * (part // rows) + h) * HEAD_DIM
                out_ref[:, at:at + HEAD_DIM] = done[h * rows:(h + 1) * rows]

    loop(1, n, lambda d: info_copy(d).wait_send())
    p1.wait_send()
    loop(1, inner, lambda d: p2_copy(d).wait_send())
    loop(1, outer, lambda d: p3_copy(d).wait_send())

    @pl.when(a + 1 < outer)
    def _():
        loop(0, a + 1, lambda f: up_copy(f).wait_send())

    loop(0, a + 1, lambda f: loop(1, inner, lambda d: side_copy(f, d).wait_send()))
    loop(0, a + 1, lambda f: loop(1, inner, lambda d: i_side(f, d).wait_send()))
    loop(0, seen, lambda j: t_mate(j).wait_send())
    loop(a + 1, outer, lambda to: i_copy(to).wait_send())
    loop(0, seen, lambda j: i_mate(j).wait_send())


def body(n, queries, text_keys, text_values, image_features, kv_weight, image_grids):
    chips = n // 2
    inner = 1
    while (2 * inner) ** 2 <= chips and chips % (2 * inner) == 0:
        inner *= 2
    outer = chips // inner
    rows, width = text_keys.shape
    kv = width // HEAD_DIM
    span = queries.shape[1] // width * rows
    slots = image_features.shape[1]
    pair = 2 * SLOTS
    j = np.arange(HEAD_DIM, dtype=np.float64) % (HEAD_DIM // 2)
    freq = jnp.asarray((1000000.0 ** (-2.0 * j / HEAD_DIM)).astype(np.float32)[None, :])
    dma = pltpu.SemaphoreType.DMA
    vmem = pl.BlockSpec(memory_space=pltpu.VMEM)
    smem = pl.BlockSpec(memory_space=pltpu.SMEM)
    hbm = pl.BlockSpec(memory_space=pl.ANY)
    lines = -(-(3 + slots // 128) // 8) * 8
    return pl.pallas_call(
        functools.partial(kernel, n, inner),
        out_shape=(
            jax.ShapeDtypeStruct(queries.shape, BF16),
            jax.ShapeDtypeStruct(text_keys.shape, BF16),
            jax.ShapeDtypeStruct(text_values.shape, BF16),
        ),
        in_specs=[hbm, vmem, vmem, hbm, hbm, smem, vmem],
        out_specs=(vmem,) * 3,
        scratch_shapes=[
            pltpu.VMEM(queries.shape, BF16),
            pltpu.VMEM(image_features.shape, BF16),
            pltpu.VMEM(kv_weight.shape, BF16),
            dma((3,)),
            pltpu.VMEM((n * rows, 2 * width), BF16),
            pltpu.VMEM((2, chips, pair, width), BF16),
            pltpu.VMEM((n, lines, 128), F32),
            pltpu.VMEM((lines, 128), F32),
            pltpu.VMEM((slots, width), F32),
            pltpu.VMEM((slots, width), BF16),
            pltpu.VMEM((slots, width), BF16),
            pltpu.VMEM((slots, width), BF16),
            pltpu.VMEM((inner, outer * pair, width), BF16),
            pltpu.VMEM((outer, pair, width), BF16),
            pltpu.VMEM((outer, pair, width), BF16),
            pltpu.VMEM((kv, span, HEAD_DIM), BF16),
            pltpu.VMEM((1, n * rows), jnp.int32),
            pltpu.VMEM((1, slots), jnp.int32),
            pltpu.VMEM((kv, span, HEAD_DIM), F32),
            pltpu.VMEM((kv, span, 2 * HEAD_DIM), F32),
            dma((n,)), dma((n,)), dma, dma, dma((inner,)), dma((inner,)), dma((outer,)), dma((outer,)),
            dma((outer,)), dma((chips,)), dma((chips,)), dma((chips,)), dma((chips,)),
            dma((outer,)), dma((chips,)), dma((chips,)), dma((chips,)), dma((chips,)),
        ],
        compiler_params=pltpu.CompilerParams(
            collective_id=0, has_side_effects=True, vmem_limit_bytes=60 * 1024 * 1024
        ),
        cost_estimate=pl.CostEstimate(
            flops=4 * n * rows * queries.size, bytes_accessed=4 * queries.size,
            transcendentals=n * rows * rows * 32),
    )(queries, text_keys, text_values, image_features, kv_weight, image_grids, freq)


def solution(mesh):
    both = P(("groups", "ctx"), None)
    return jax.shard_map(
        functools.partial(body, mesh.shape["ctx"]), mesh=mesh,
        in_specs=(both, both, both, both, P("ctx", None), both),
        out_specs=(both, both, both), check_vma=False)
```

```python
import functools
import math

import jax
import jax.numpy as jnp
import numpy as np
from jax import lax
from jax.experimental import pallas as pl
from jax.experimental.pallas import tpu as pltpu
from jax.sharding import PartitionSpec as P

HEAD_DIM = 128
GRID = 4
SLOTS = GRID * GRID
BIG = 1 << 30
NEG = -1e30
F32 = jnp.float32
BF16 = jnp.bfloat16


def dot(x, y, cx, cy):
    return lax.dot_general(x, y, (((cx,), (cy,)), ((), ())), preferred_element_type=F32)


def kernel(
    n, inner,
    q_hbm, tk_ref, tv_ref, feat_hbm, w_hbm, grid_ref, freq_ref,
    out_ref, ck_ref, cv_ref,
    q_ref, feat_ref, w_ref, load_s, tkv, img, info, info_sum, mine, p1_src, p1_dst, p2_src, p2_dst, p3_src, p3_dst, qs, pos_t, pos_i, m_ref, acc_ref,
    info_s, info_r, p1_s, p1_r, p2_s, p2_r, p3_s, p3_r,
    tz_s, ty_s, t_r, tm_s, tm_r, i_s, is_s, i_r, im_s, im_r,
):
    chips = n // 2
    outer = chips // inner
    rows, width = tk_ref.shape
    kv = width // HEAD_DIM
    group = q_ref.shape[1] // width
    feats, slots = feat_ref.shape
    pair = 2 * SLOTS
    total_features = feats * n
    me = lax.axis_index("ctx")
    core = lax.rem(me, 2)
    chip = me // 2
    a = chip // inner
    b = lax.rem(chip, inner)
    mate = me + 1 - 2 * core

    def loop(low, high, f):
        lax.fori_loop(low, high, lambda i, c: (f(i), c)[1], 0)

    def copy(src, dst, send, recv, target):
        return pltpu.make_async_remote_copy(
            src_ref=src, dst_ref=dst, send_sem=send, recv_sem=recv,
            device_id={"ctx": target}, device_id_type=pl.DeviceIdType.MESH,
        )

    loads = [pltpu.make_async_copy(src, dst, load_s.at[i]) for i, (src, dst) in enumerate(
        ((feat_hbm, feat_ref), (w_hbm, w_ref), (q_hbm, q_ref)))]
    for load in loads:
        load.start()

    own = pl.ds(pl.multiple_of(me * rows, rows), rows)
    tkv[:, width:] = jnp.zeros((n * rows, width), BF16)
    tkv[own, :width] = tk_ref[...]
    tkv[own, width:] = tv_ref[...]
    offset, tall, wide = grid_ref[0, 0], grid_ref[0, 1], grid_ref[0, 2]
    img[...] = jnp.zeros_like(img)

    barrier = pltpu.get_barrier_semaphore()
    loop(1, n, lambda d: pl.semaphore_signal(
        barrier, inc=1, device_id={"ctx": lax.rem(me + d, n)},
        device_id_type=pl.DeviceIdType.MESH))
    pl.semaphore_wait(barrier, n - 1)

    def block(j):
        shard = 2 * j + core
        return tkv.at[pl.ds(pl.multiple_of(shard * rows, rows), rows), :]

    def info_copy(d):
        return copy(info.at[me], info.at[me], info_s.at[d], info_r.at[me], lax.rem(me + d, n))

    def info_in(j):
        return copy(info.at[j], info.at[j], info_s.at[0], info_r.at[j], mate)

    def up_copy(from_a):
        j = from_a * inner + b
        return copy(block(j), block(j), tz_s.at[from_a], t_r.at[j], me + 2 * inner)

    def side_copy(from_a, d):
        j = from_a * inner + b
        return copy(block(j), block(j), ty_s.at[from_a * inner + d], t_r.at[j],
                    2 * (a * inner + lax.rem(b + d, inner)) + core)

    def t_in(j):
        return copy(block(j), block(j), tz_s.at[0], t_r.at[j], mate)

    def t_mate(j):
        return copy(block(j), block(j), tm_s.at[j], tm_r.at[j], mate)

    def t_mate_in(j):
        shard = 2 * j + 1 - core
        ref = tkv.at[pl.ds(pl.multiple_of(shard * rows, rows), rows), :]
        return copy(ref, ref, tm_s.at[j], tm_r.at[j], mate)

    @pl.when(a + 1 < outer)
    def _():
        up_copy(a).start()

    loop(1, inner, lambda d: side_copy(a, d).start())
    t_mate(chip).start()

    half = lambda c: w_ref[:, pl.ds(pl.multiple_of(c * width, width), width)]
    loads[0].wait()
    features = feat_ref[...].T
    loads[1].wait()
    p1_src[...] = dot(features, half(1 - core), 1, 0).astype(BF16)
    p1 = copy(p1_src, p1_dst, p1_s, p1_r, mate)
    p1.start()
    mine[...] = dot(features, half(core), 1, 0)

    p1.wait_recv()
    both_cores = mine[...] + p1_dst[...].astype(F32)
    mine[...] = both_cores
    for j in range(chips):
        to = (j % inner * outer + j // inner) * pair
        p2_src[to:to + pair, :] = both_cores[j * pair:(j + 1) * pair].astype(BF16)

    def pass_on(i):
        from_a = a - 1 - i
        j = from_a * inner + b
        t_in(j).wait_recv()

        @pl.when(a + 1 < outer)
        def _():
            up_copy(from_a).start()

        loop(1, inner, lambda d: side_copy(from_a, d).start())
        t_mate(j).start()

    first_on = jnp.minimum(a, 1)

    column = outer * pair

    def p2_copy(d):
        to_b = lax.rem(b + d, inner)
        return copy(p2_src.at[pl.ds(pl.multiple_of(to_b * column, column), column), :],
                    p2_dst.at[b], p2_s.at[d], p2_r.at[b], 2 * (a * inner + to_b) + core)

    def p2_in(j):
        return copy(p2_dst.at[j], p2_dst.at[j], p2_s.at[0], p2_r.at[j], mate)

    def p3_copy(d):
        to_a = lax.rem(a + d, outer)
        return copy(p3_src.at[to_a], p3_dst.at[a], p3_s.at[d], p3_r.at[a],
                    2 * (to_a * inner + b) + core)

    def p3_in(j):
        return copy(p3_dst.at[j], p3_dst.at[j], p3_s.at[0], p3_r.at[j], mate)

    def column_sum(of_a):
        at = pl.ds(pl.multiple_of((of_a * inner + b) * pair, pair), pair)
        total = mine[at, :]
        at = pl.ds(pl.multiple_of(of_a * pair, pair), pair)
        return lax.fori_loop(
            1, inner,
            lambda d, x: x + p2_dst[lax.rem(b + d, inner), at, :].astype(F32), total)

    loop(1, inner, lambda d: p2_copy(d).start())
    loop(0, first_on, pass_on)

    wide_f = feat_ref[...].astype(F32)
    power = jnp.sum(wide_f * wide_f, axis=0, keepdims=True)
    line = lax.broadcasted_iota(jnp.int32, info.shape[1:], 0)
    facts = jnp.where(line == 0, offset, jnp.where(line == 1, tall, wide)).astype(F32)
    for i in range(slots // 128):
        facts = jnp.where(line == 3 + i, power[:, i * 128:(i + 1) * 128], facts)
    info[me] = facts
    loop(1, n, lambda d: info_copy(d).start())

    loop(1, inner, lambda d: p2_in(lax.rem(b + d, inner)).wait_recv())

    def send_sum(d):
        to_a = lax.rem(a + d, outer)
        p3_src[to_a] = column_sum(to_a).astype(BF16)
        p3_copy(d).start()

    loop(1, outer, send_sum)

    loads[2].wait()
    for g in range(kv):
        for h in range(group):
            at = (g * group + h) * HEAD_DIM
            qs[g, h * rows:(h + 1) * rows, :] = q_ref[:, at:at + HEAD_DIM]

    def gather_facts(d, total):
        j = lax.rem(me + d, n)
        info_in(j).wait_recv()
        return total + info[j]

    info_sum[...] = lax.fori_loop(1, n, gather_facts, info[me])

    row = lax.broadcasted_iota(jnp.int32, (pair, 128), 0)
    lane = lax.broadcasted_iota(jnp.int32, (pair, 128), 1)
    second = row >= SLOTS
    k = jnp.where(second, row - SLOTS, row)
    pick = lambda i: jnp.where(
        second, info[2 * chip + 1, i:i + 1, :], info[2 * chip, i:i + 1, :]).astype(jnp.int32)
    gw = pick(2)
    gy = jnp.zeros_like(k)
    for i in range(1, SLOTS // 2):
        gy = gy + jnp.where(k >= i * gw, 1, 0)
    gx = k - gy * gw
    t_id = (2 * chip + jnp.where(second, 1, 0)) * rows + pick(0)
    j = jnp.where(lane >= HEAD_DIM // 2, lane - HEAD_DIM // 2, lane)
    first_bound = HEAD_DIM // 8
    second_bound = first_bound + 3 * HEAD_DIM // 16
    ids = t_id + jnp.where(j < first_bound, 0, jnp.where(j < second_bound, gy, gx))
    angle = ids.astype(F32) * freq_ref[...]
    is_key = core == 0
    cosine = jnp.where(is_key, jnp.cos(angle), 1.0)
    sine = jnp.where(is_key, jnp.sin(angle), 0.0)
    sine = jnp.where(lane < HEAD_DIM // 2, -sine, sine)

    loop(first_on, a, pass_on)

    lane_t = lax.broadcasted_iota(jnp.int32, pos_t.shape, 1)
    lane_i = lax.broadcasted_iota(jnp.int32, pos_i.shape, 1)
    shard_t = lane_t // rows
    shard_i = lane_i // SLOTS

    def place(j, carry):
        text, image = carry
        code = info[j, 0:1, :] * 64.0 + info[j, 1:2, :] * info[j, 2:3, :]
        spread = lambda x: jnp.concatenate([code] * (x.shape[1] // 128), axis=1)
        return (jnp.where(shard_t == j, spread(text), text),
                jnp.where(shard_i == j, spread(image), image))

    text, image = lax.fori_loop(
        0, n, place, (jnp.zeros(pos_t.shape, F32), jnp.zeros(pos_i.shape, F32)))
    text, image = text.astype(jnp.int32), image.astype(jnp.int32)
    within = lane_t - shard_t * rows - text // 64
    pos_t[...] = jnp.where((within >= 0) & (within < text % 64), BIG, lane_t)
    within = lane_i - shard_i * SLOTS
    pos_i[...] = jnp.where(
        within < image % 64, shard_i * rows + image // 64 + within, BIG)

    def add(d, total):
        src = lax.rem(a + d, outer)
        p3_in(src).wait_recv()
        return total + p3_dst[src].astype(F32)

    total = lax.fori_loop(1, outer, add, column_sum(a))
    squares = info_sum[pl.ds(3 + chip * pair // 128, 1), :]
    squares = jnp.where(lane == lax.rem(chip * pair, 128) + row, squares, 0.0)
    power = jnp.sum(squares, axis=1, keepdims=True)
    scale = lax.rsqrt(power / total_features + 1e-6)
    for h in range(kv):
        at = slice(h * HEAD_DIM, (h + 1) * HEAD_DIM)
        x = total[:, at] * scale
        turned = jnp.concatenate([x[:, HEAD_DIM // 2:], x[:, :HEAD_DIM // 2]], axis=1)
        img[core, chip, :, at] = (x * cosine + turned * sine).astype(BF16)

    def i_copy(to_a):
        return copy(img.at[core, chip], img.at[core, chip], i_s.at[to_a], i_r.at[chip],
                    2 * (to_a * inner + b) + core)

    def i_side(from_a, d):
        j = from_a * inner + b
        return copy(img.at[core, j], img.at[core, j], is_s.at[from_a * inner + d], i_r.at[j],
                    2 * (a * inner + lax.rem(b + d, inner)) + core)

    def i_in(j):
        return copy(img.at[core, j], img.at[core, j], i_s.at[0], i_r.at[j], mate)

    def i_mate(j):
        return copy(img.at[core, j], img.at[core, j], im_s.at[j], im_r.at[j], mate)

    def i_mate_in(j):
        return copy(img.at[1 - core, j], img.at[1 - core, j], im_s.at[j], im_r.at[j], mate)

    seen = (a + 1) * inner
    loop(a + 1, outer, lambda to: i_copy(to).start())
    loop(1, inner, lambda d: i_side(a, d).start())
    i_mate(chip).start()
    def from_side(from_a):
        def step(d):
            j = from_a * inner + lax.rem(b + d, inner)
            t_in(j).wait_recv()
            t_mate(j).start()

        loop(1, inner, step)

    span = group * rows
    part = math.gcd(span, 256)
    plane = 2 * inner * rows
    block_keys = max(plane, math.gcd(n * rows, 512))
    planes = block_keys // plane
    last = a // planes
    factor = math.log2(math.e) / math.sqrt(HEAD_DIM)
    q_pos = me * rows + lax.rem(lax.broadcasted_iota(jnp.int32, (part, 1), 0), rows)

    def attend(g, r, keys, values, pos, first):
        at = slice(r * part, (r + 1) * part)
        s = dot(qs[g, at, :], keys, 1, 1)
        s = jnp.where(pos <= q_pos, s, NEG)
        now = jnp.broadcast_to(jnp.max(s, axis=1, keepdims=True), (part, HEAD_DIM))
        if not first:
            before = m_ref[g, at, :]
            now = jnp.maximum(before, now)
        shift = jnp.concatenate([now] * (s.shape[1] // HEAD_DIM), axis=1)
        weight = jnp.exp2((s - shift) * factor).astype(BF16)
        both = jnp.concatenate([values, jnp.ones_like(values)], axis=1)
        product = dot(weight, both, 1, 0)
        summed, totals = product[:, :HEAD_DIM], product[:, HEAD_DIM:]
        if not first:
            shrink = jnp.exp2((before - now) * factor)
            summed = summed + acc_ref[g, at, :HEAD_DIM] * shrink
            totals = totals + acc_ref[g, at, HEAD_DIM:] * shrink
        return now, summed, totals

    def text_block(g, r, p, first):
        at = pl.ds(pl.multiple_of(p * block_keys, block_keys), block_keys)
        lo = g * HEAD_DIM
        now, summed, totals = attend(
            g, r, tkv[at, lo:lo + HEAD_DIM], tkv[at, width + lo:width + lo + HEAD_DIM],
            pos_t[:, at], first)
        at = slice(r * part, (r + 1) * part)
        m_ref[g, at, :] = now
        acc_ref[g, at, :HEAD_DIM] = summed
        acc_ref[g, at, HEAD_DIM:] = totals

    def text_heads(heads, p, first):
        for g in heads:
            for r in range(span // part):
                text_block(g, r, p, first)

    def text_wait(p):
        low = p * planes * inner
        high = jnp.minimum(seen, low + planes * inner)
        loop(low, high, lambda j: t_mate_in(j).wait_recv())

    def image_on(from_a):
        j = from_a * inner + b
        i_in(j).wait_recv()
        loop(1, inner, lambda d: i_side(from_a, d).start())
        i_mate(j).start()

    def image_from_side(from_a):
        def step(d):
            j = from_a * inner + lax.rem(b + d, inner)
            i_in(j).wait_recv()
            i_mate(j).start()

        loop(1, inner, step)

    def images_on():
        loop(0, a, image_on)

    def images_from_side():
        loop(0, a + 1, image_from_side)

    low = last * planes
    loop(0, a + 1 - low, lambda i: from_side(a - i))
    text_wait(last)
    text_heads(range(kv // 2), last, True)
    loop(0, low, lambda i: from_side(low - 1 - i))
    text_heads(range(kv // 2, kv - 1), last, True)
    images_on()
    text_heads(range(kv - 1, kv), last, True)

    def more(i):
        p = last - 1 - i
        text_wait(p)
        text_heads(range(kv // 2), p, False)

        @pl.when(p == 0)
        def _():
            images_from_side()

        text_heads(range(kv // 2, kv), p, False)

    loop(0, last, more)

    @pl.when(last == 0)
    def _():
        images_from_side()

    loop(0, seen, lambda j: i_mate_in(j).wait_recv())
    local = lax.broadcasted_iota(jnp.int32, (rows, SLOTS), 0)
    within = lax.broadcasted_iota(jnp.int32, (rows, SLOTS), 1)
    count = tall * wide
    hot = jnp.where((local == offset + within) & (within < count), 1.0, 0.0).astype(BF16)
    local = lax.broadcasted_iota(jnp.int32, (rows, width), 0)
    is_image = (local >= offset) & (local < offset + count)
    mine_slots = pl.ds(pl.multiple_of(core * SLOTS, SLOTS), SLOTS)
    for c, (ref, text_ref) in enumerate(((ck_ref, tk_ref), (cv_ref, tv_ref))):
        placed = dot(hot, img[c, chip, mine_slots, :], 1, 0)
        ref[...] = jnp.where(is_image, placed, text_ref[...].astype(F32)).astype(BF16)
    for g in range(kv):
        lanes = slice(g * HEAD_DIM, (g + 1) * HEAD_DIM)
        keys = img[0, :, :, lanes].reshape(slots, HEAD_DIM)
        values = img[1, :, :, lanes].reshape(slots, HEAD_DIM)
        for r in range(span // part):
            now, summed, totals = attend(g, r, keys, values, pos_i[...], False)
            done = (summed / totals).astype(BF16)
            for h in range(part // rows):
                at = (g * group + r * (part // rows) + h) * HEAD_DIM
                out_ref[:, at:at + HEAD_DIM] = done[h * rows:(h + 1) * rows]

    loop(1, n, lambda d: info_copy(d).wait_send())
    p1.wait_send()
    loop(1, inner, lambda d: p2_copy(d).wait_send())
    loop(1, outer, lambda d: p3_copy(d).wait_send())

    @pl.when(a + 1 < outer)
    def _():
        loop(0, a + 1, lambda f: up_copy(f).wait_send())

    loop(0, a + 1, lambda f: loop(1, inner, lambda d: side_copy(f, d).wait_send()))
    loop(0, a + 1, lambda f: loop(1, inner, lambda d: i_side(f, d).wait_send()))
    loop(0, seen, lambda j: t_mate(j).wait_send())
    loop(a + 1, outer, lambda to: i_copy(to).wait_send())
    loop(0, seen, lambda j: i_mate(j).wait_send())


def body(n, queries, text_keys, text_values, image_features, kv_weight, image_grids):
    chips = n // 2
    inner = 1
    while (2 * inner) ** 2 <= chips and chips % (2 * inner) == 0:
        inner *= 2
    outer = chips // inner
    rows, width = text_keys.shape
    kv = width // HEAD_DIM
    span = queries.shape[1] // width * rows
    slots = image_features.shape[1]
    pair = 2 * SLOTS
    j = np.arange(HEAD_DIM, dtype=np.float64) % (HEAD_DIM // 2)
    freq = jnp.asarray((1000000.0 ** (-2.0 * j / HEAD_DIM)).astype(np.float32)[None, :])
    dma = pltpu.SemaphoreType.DMA
    vmem = pl.BlockSpec(memory_space=pltpu.VMEM)
    smem = pl.BlockSpec(memory_space=pltpu.SMEM)
    hbm = pl.BlockSpec(memory_space=pl.ANY)
    lines = -(-(3 + slots // 128) // 8) * 8
    return pl.pallas_call(
        functools.partial(kernel, n, inner),
        out_shape=(
            jax.ShapeDtypeStruct(queries.shape, BF16),
            jax.ShapeDtypeStruct(text_keys.shape, BF16),
            jax.ShapeDtypeStruct(text_values.shape, BF16),
        ),
        in_specs=[hbm, vmem, vmem, hbm, hbm, smem, vmem],
        out_specs=(vmem,) * 3,
        scratch_shapes=[
            pltpu.VMEM(queries.shape, BF16),
            pltpu.VMEM(image_features.shape, BF16),
            pltpu.VMEM(kv_weight.shape, BF16),
            dma((3,)),
            pltpu.VMEM((n * rows, 2 * width), BF16),
            pltpu.VMEM((2, chips, pair, width), BF16),
            pltpu.VMEM((n, lines, 128), F32),
            pltpu.VMEM((lines, 128), F32),
            pltpu.VMEM((slots, width), F32),
            pltpu.VMEM((slots, width), BF16),
            pltpu.VMEM((slots, width), BF16),
            pltpu.VMEM((slots, width), BF16),
            pltpu.VMEM((inner, outer * pair, width), BF16),
            pltpu.VMEM((outer, pair, width), BF16),
            pltpu.VMEM((outer, pair, width), BF16),
            pltpu.VMEM((kv, span, HEAD_DIM), BF16),
            pltpu.VMEM((1, n * rows), jnp.int32),
            pltpu.VMEM((1, slots), jnp.int32),
            pltpu.VMEM((kv, span, HEAD_DIM), F32),
            pltpu.VMEM((kv, span, 2 * HEAD_DIM), F32),
            dma((n,)), dma((n,)), dma, dma, dma((inner,)), dma((inner,)), dma((outer,)), dma((outer,)),
            dma((outer,)), dma((chips,)), dma((chips,)), dma((chips,)), dma((chips,)),
            dma((outer,)), dma((chips,)), dma((chips,)), dma((chips,)), dma((chips,)),
        ],
        compiler_params=pltpu.CompilerParams(
            collective_id=0, has_side_effects=True, vmem_limit_bytes=60 * 1024 * 1024
        ),
        cost_estimate=pl.CostEstimate(
            flops=4 * n * rows * queries.size, bytes_accessed=4 * queries.size,
            transcendentals=n * rows * rows * 32),
    )(queries, text_keys, text_values, image_features, kv_weight, image_grids, freq)


def solution(mesh):
    both = P(("groups", "ctx"), None)
    return jax.shard_map(
        functools.partial(body, mesh.shape["ctx"]), mesh=mesh,
        in_specs=(both, both, both, both, P("ctx", None), both),
        out_specs=(both, both, both), check_vma=False)
```
